128 devices in a mesh: fsdp: 32 (over z_hi, x, y), rep: 4 (over z_lo, core).
Axes of the slice: x: 4, y: 4, z: 4 (z_hi: 2, z_lo: 2; z = z_hi * 2 + z_lo), core: 2. Of those that a mesh axis runs over, the one named last changes fastest.
Arguments:
- tokens: bfloat16 [20480, 1088], P(('fsdp', 'rep')), may hold values from -6 to 6
- lengths: int32 [128, 4], P(('fsdp', 'rep')), may hold values from 1 to 100, 160 in all within a row
- cotangent: bfloat16 [20480, 1088], P(('fsdp', 'rep')), may hold values from -6 to 6
- attn_gain: bfloat16 [1088], P('fsdp'), may hold values from 0.099609375 to 1.8984375
- attn_shift: bfloat16 [1088], P('fsdp'), may hold values from -3 to 3
- qkv_weight: bfloat16 [1088, 3264], P('fsdp'), may hold values from -0.1875 to 0.1875
- query_bias: bfloat16 [1088], P('fsdp'), may hold values from -3 to 3
- value_bias: bfloat16 [1088], P('fsdp'), may hold values from -3 to 3
- out_weight: bfloat16 [1088, 1088], P('fsdp'), may hold values from -0.625 to 0.625
- out_bias: bfloat16 [1088], P('fsdp'), may hold values from -3 to 3
- mlp_gain: bfloat16 [1088], P('fsdp'), may hold values from 0.099609375 to 1.8984375
- mlp_shift: bfloat16 [1088], P('fsdp'), may hold values from -3 to 3
- up_weight: bfloat16 [1088, 4352], P('fsdp'), may hold values from -0.1875 to 0.1875
- up_bias: bfloat16 [4352], P('fsdp'), may hold values from -3 to 3
- down_weight: bfloat16 [4352, 1088], P('fsdp'), may hold values from -0.09375 to 0.09375
- down_bias: bfloat16 [1088], P('fsdp'), may hold values from -3 to 3
Outputs:
- layer_out: bfloat16 [20480, 1088], P(('fsdp', 'rep'))
- input_grad: float32 [20480, 1088], P(('fsdp', 'rep'))
- attn_gain_grad: float32 [1088], P('fsdp')
- attn_shift_grad: float32 [1088], P('fsdp')
- qkv_weight_grad: float32 [1088, 3264], P('fsdp')
- query_bias_grad: float32 [1088], P('fsdp')
- value_bias_grad: float32 [1088], P('fsdp')
- out_weight_grad: float32 [1088, 1088], P('fsdp')
- out_bias_grad: float32 [1088], P('fsdp')
- mlp_gain_grad: float32 [1088], P('fsdp')
- mlp_shift_grad: float32 [1088], P('fsdp')
- up_weight_grad: float32 [1088, 4352], P('fsdp')
- up_bias_grad: float32 [4352], P('fsdp')
- down_weight_grad: float32 [4352, 1088], P('fsdp')
- down_bias_grad: float32 [1088], P('fsdp')
The draws below stay inside these ranges and needn't reach their ends.
Inputs may be any that keep to these rules, and one draw needn't show every extreme that they name: Each row of 4 lengths sums to 160 and gives one device's sequences in order; in every row the longest is exactly 100.
All inputs are finite; a program needn't handle non-finite values.
Results may differ from the reference program's by a relative error of at most 0.011.
Values may be sent and summed in bfloat16 or wider, within the bound.
A program may use at most 192 MiB of HBM per device.

```python
import math
import jax
import jax.numpy as jnp
import numpy as np
from jax import lax

HEADS = 17
HEAD_DIM = 64
FF = 4352
D = 1088
TOK_DEV = 160
SEQS_DEV = 4
LONGEST = 100
TOKENS = 20480
DEVICES = 128


def shard_levels(key, shape, pieces, least, top_value):
    def one(dim, shards_of):
        heights = jax.random.uniform(jax.random.fold_in(jax.random.fold_in(key, 6), dim), (shards_of,), jnp.float32, least / len(pieces), top_value / len(pieces))
        return jnp.repeat(jnp.exp(heights), shape[dim] // shards_of).reshape((-1,) + (1,) * (len(shape) - dim - 1))

    factor_of = one(*pieces[0])
    for cut in pieces[1:]:
        factor_of = factor_of * one(*cut)
    return factor_of


def length_profile(number_of, total, bound, skew):
    portions = [(1 << 20) // math.isqrt(standing ** skew) + 1 for standing in range(2, number_of + 1)]
    rest, counts = total - bound - (number_of - 1), [1] * (number_of - 1)
    while rest > 0:
        candidates = [i for i in range(number_of - 1) if counts[i] < bound]
        pool, remaining = sum([portions[i] for i in candidates]), rest
        for i in candidates:
            extra = min(bound - counts[i], max(1, remaining * portions[i] // pool), rest)
            counts[i] = counts[i] + extra
            rest = rest - extra
    return np.array([bound] + counts)


def ragged_sizes(own_key, amount, total, limit, lean):
    if amount == 2:
        one = jax.random.randint(own_key, (), max(1, total - limit), min(limit, total - 1) + 1)
        return jnp.stack([one, total - one])
    tallies = jnp.asarray(length_profile(amount, total, limit, lean), jnp.int32)
    couples = (amount - 1) // 2
    giver, taker = tallies[1:1 + 2 * couples:2], tallies[2:2 + 2 * couples:2]
    slack = jnp.minimum(giver - 1, limit - taker)
    shifted = jax.random.randint(jax.random.fold_in(own_key, 1), (couples,), 0, 1 << 20) % (slack + 1)
    tallies = tallies.at[1:1 + 2 * couples:2].set(giver - shifted).at[2:2 + 2 * couples:2].set(taker + shifted)
    return tallies[jax.random.permutation(jax.random.fold_in(own_key, 2), amount)]


def normal_values(key, shape, scale, most, pieces=(), held_as=jnp.bfloat16):
    array = jax.random.normal(key, shape, jnp.float32) * scale
    if len(pieces) > 0:
        array = shard_levels(key, shape, pieces, -0.22, 0.18) * array
    return jnp.clip(array, min=-most, max=most).astype(held_as)


def setup_inputs(seed: int = 0) -> dict:
    seeds = jax.random.split(jax.random.key(seed), 17)
    tokens = normal_values(seeds[0], (TOKENS, D), 1.0, 6.0, ((0, 128),))
    lengths = jax.vmap(lambda own: ragged_sizes(own, SEQS_DEV, TOK_DEV, LONGEST, 2))(jax.random.split(seeds[1], DEVICES)).reshape((DEVICES, SEQS_DEV)).astype(jnp.int32)
    cotangent = normal_values(seeds[2], (TOKENS, D), 1.0, 6.0, ((0, 128),))
    attn_gain = jnp.clip(1.0 + 0.18 * jax.random.normal(seeds[3], (D,), jnp.float32), 0.099609375, 1.8984375).astype(jnp.bfloat16)
    attn_shift = normal_values(seeds[4], (D,), 0.5, 3.0, ((0, 32),))
    qkv_weight = normal_values(seeds[5], (D, 3 * D), D ** -0.5, 0.1875, ((0, 32),))
    query_bias = normal_values(seeds[6], (D,), 0.5, 3.0, ((0, 32),))
    value_bias = normal_values(seeds[7], (D,), 0.5, 3.0, ((0, 32),))
    out_weight = normal_values(seeds[8], (D, D), (D * 16 // TOK_DEV) ** -0.5, 0.625, ((0, 32),))
    out_bias = normal_values(seeds[9], (D,), 0.5, 3.0, ((0, 32),))
    mlp_gain = jnp.clip(1.0 + 0.18 * jax.random.normal(seeds[10], (D,), jnp.float32), 0.099609375, 1.8984375).astype(jnp.bfloat16)
    mlp_shift = normal_values(seeds[11], (D,), 0.5, 3.0, ((0, 32),))
    up_weight = normal_values(seeds[12], (D, FF), D ** -0.5, 0.1875, ((0, 32),))
    up_bias = normal_values(seeds[13], (FF,), 0.5, 3.0, ((0, 32),))
    down_weight = normal_values(seeds[14], (FF, D), FF ** -0.5, 0.09375, ((0, 32),))
    down_bias = normal_values(seeds[15], (D,), 0.5, 3.0, ((0, 32),))
    return dict(tokens=tokens, lengths=lengths, cotangent=cotangent, attn_gain=attn_gain, attn_shift=attn_shift, qkv_weight=qkv_weight, query_bias=query_bias, value_bias=value_bias, out_weight=out_weight, out_bias=out_bias, mlp_gain=mlp_gain, mlp_shift=mlp_shift, up_weight=up_weight, up_bias=up_bias, down_weight=down_weight, down_bias=down_bias)


@jax.custom_vjp
def low(v):
    return lax.optimization_barrier(v.astype(jnp.bfloat16)).astype(jnp.float32)

@jax.custom_vjp
def low_back(v):
    return v

def low_keep(v):
    return (low(v), None)

def low_pass(kept, grad):
    return (grad,)

def back_keep(v):
    return (v, None)

def back_low(kept, grad):
    return (low(grad),)
low.defvjp(low_keep, low_pass)
low_back.defvjp(back_keep, back_low)
epsilon = 1e-05
excluded = -1000000000.0

def layer_norm(values, norm_gain, norm_shift):
    average = lax.optimization_barrier(jnp.mean(values, axis=-1, keepdims=True))
    centered = values - average
    variance = lax.optimization_barrier(jnp.mean(centered * centered, axis=-1, keepdims=True))
    return centered * lax.rsqrt(variance + epsilon) * norm_gain + norm_shift

def gelu_tanh(values):
    return jax.nn.gelu(values, approximate=True)

def causal_segments(seq_lengths, count):
    ends = jnp.cumsum(seq_lengths.astype(jnp.int32)).astype(jnp.int32)
    position = jnp.arange(count, dtype=jnp.int32)
    segment = lax.optimization_barrier(jnp.sum((position[:, None] >= ends[None, :]).astype(jnp.int32), axis=1))
    return (segment[:, None] == segment[None, :]) & (position[:, None] >= position[None, :])

def head_split(rows):
    return rows.reshape(rows.shape[0], HEADS, HEAD_DIM)

def block_forward(weights, inputs, seq_lengths):
    gain_first, shift_first, qkv_full, query_shift, value_shift, out_full, out_shift, gain_second, shift_second, up_full, up_shift, down_full, down_shift = weights
    count, width = inputs.shape
    highest = lax.Precision.HIGHEST
    normed_first = low(layer_norm(inputs, gain_first, shift_first))
    projected = jnp.dot(normed_first, qkv_full, precision=highest)
    query_heads = head_split(low(low_back(projected[:, :width] + query_shift)))
    key_heads = head_split(low(low_back(projected[:, width:2 * width])))
    value_heads = head_split(low(low_back(projected[:, 2 * width:] + value_shift)))
    scores = low_back(jnp.einsum('qhd,khd->hqk', query_heads, key_heads, precision=highest) * HEAD_DIM ** (-0.5))
    allowed = causal_segments(seq_lengths, count)
    probs = jax.nn.softmax(jnp.where(allowed[None], scores, excluded), axis=-1)
    mixed = jnp.einsum('hqk,khd->qhd', low(probs), value_heads, precision=highest)
    attended = low(low_back(mixed.reshape(count, width)))
    resid = inputs + low_back(jnp.dot(attended, out_full, precision=highest) + out_shift)
    normed_second = low(layer_norm(resid, gain_second, shift_second))
    hidden = low_back(jnp.dot(normed_second, up_full, precision=highest) + up_shift)
    activated = low(gelu_tanh(hidden))
    return resid + low_back(jnp.dot(activated, down_full, precision=highest) + down_shift)

def reference(tokens, lengths, cotangent, attn_gain, attn_shift, qkv_weight, query_bias, value_bias, out_weight, out_bias, mlp_gain, mlp_shift, up_weight, up_bias, down_weight, down_bias):
    weights = (attn_gain.astype(jnp.float32), attn_shift.astype(jnp.float32), qkv_weight.astype(jnp.float32), query_bias.astype(jnp.float32), value_bias.astype(jnp.float32), out_weight.astype(jnp.float32), out_bias.astype(jnp.float32), mlp_gain.astype(jnp.float32), mlp_shift.astype(jnp.float32), up_weight.astype(jnp.float32), up_bias.astype(jnp.float32), down_weight.astype(jnp.float32), down_bias.astype(jnp.float32))
    blocks = lengths.shape[0]
    inputs = tokens.astype(jnp.float32).reshape(blocks, TOK_DEV, tokens.shape[1])
    checked = jax.checkpoint(block_forward)

    def whole(weight_set, block_inputs):

        def one_block(pair):
            return checked(weight_set, pair[0], pair[1])
        return lax.map(one_block, (block_inputs, lengths))
    outputs, pullback = jax.vjp(whole, weights, inputs)
    weight_grads, input_grads = pullback(cotangent.astype(jnp.float32).reshape(outputs.shape))
    return (outputs.reshape(tokens.shape).astype(jnp.bfloat16), input_grads.reshape(tokens.shape), weight_grads[0], weight_grads[1], weight_grads[2], weight_grads[3], weight_grads[4], weight_grads[5], weight_grads[6], weight_grads[7], weight_grads[8], weight_grads[9], weight_grads[10], weight_grads[11], weight_grads[12])
```

```python
import functools

import jax
import jax.numpy as jnp
from jax import lax
from jax.experimental import pallas as pl
from jax.experimental.pallas import tpu as pltpu
from jax.sharding import PartitionSpec as P

MESH = pl.DeviceIdType.MESH
AXES = "xyz"
ORDERS = ("xyz", "yzx", "zxy")

def place():
    f = lax.axis_index("fsdp"); r = lax.axis_index("rep")
    return dict(x=(f // 4) % 4, y=f % 4, z=(f // 16) * 2 + r // 2), r % 2

def device(at, core):
    z = at["z"]
    return ((z // 2) * 16 + at["x"] * 4 + at["y"], (z % 2) * 2 + core)

def moved(at, axis, step):
    return {**at, axis: lax.rem(at[axis] + step + 4, 4)}

def slot(ref, at, core, cols, kind):
    z = at["z"]
    every = slice(None)
    zh, zl = (every, every) if z is None else (z // 2, lax.rem(z, 2))
    x = every if at["x"] is None else at["x"]
    y = every if at["y"] is None else at["y"]
    if kind == "cols":
        return ref.at[zh, x, y, zl, :, pl.ds(pl.multiple_of(core * 2176 + cols[0], 128), cols[1])]
    return ref.at[zh, x, y, zl, core, :, pl.ds(cols[0], cols[1])]

def units():
    out = [(3, 0, 0, 256, 256)]
    for w in (0, 1):
        out += [(w, 0, 0, 384, 384), (w, 1, 768, 384, 384), (w, 2, 1536, 384, 256)]
    out += [(2, 0, 0, 256, 128), (2, 1, 384, 256, 128), (2, 2, 768, 128, 192)]
    return out
CHUNK = {3: 0, 0: 0, 1: 1, 2: 2}

def gather_kernel(sib, p0, p1, p2, p3, g0, g1, g2, g3, send, recv, ssend, srecv, lsem):
    at, core = place()
    ins, outs = (p0, p1, p2, p3), (g0, g1, g2, g3)
    me = device(at, core)
    sibling = device(at, 1 - core)
    near = {(a, s): device(moved(at, a, s), core) for a in AXES for s in (1, -1)}
    barrier = pltpu.get_barrier_semaphore()
    for d in list(near.values()) + [sibling]:
        pl.semaphore_signal(barrier, inc=1, device_id=d, device_id_type=MESH)
    pl.semaphore_wait(barrier, 7)
    U = units()
    locals_ = []
    for w in range(4):
        kind = "cols" if w < 2 else "rows"
        width = (2176, 2176, 1088, 512)[w]
        c = pltpu.make_async_copy(ins[w], slot(outs[w], at, core, (0, width), kind), lsem.at[w])
        c.start(); locals_.append(c)
    pending = []
    def block(u, phase, pos):
        order = ORDERS[U[u][1]]
        idx = dict(at)
        for a in order[:phase]:
            idx[a] = None
        idx[order[phase]] = pos
        return idx
    def copy(u, idx, cols, dst_dev, s, r, src=None):
        w = U[u][0]
        kind = "cols" if w < 2 else "rows"
        ref = slot(outs[w], idx, core, cols, kind)
        return pltpu.make_async_remote_copy(src_ref=ref if src is None else src, dst_ref=ref, send_sem=s, recv_sem=r, device_id=dst_dev, device_id_type=MESH)
    state = {}
    def sub(u, k):
        w, g, c0, h0, h1 = U[u]
        phase, b = divmod(k, 2)
        axis = ORDERS[g][phase]
        pos = at[axis]
        plus, minus = near[(axis, 1)], near[(axis, -1)]
        pp, pm, po = (lax.rem(pos + i, 4) for i in (1, 3, 2))
        own = block(u, phase, pos)
        full, A, B = (c0, h0 + h1), (c0, h0), (c0 + h0, h1)
        sem = lambda i: (send.at[u, phase, i], recv.at[u, phase, i])
        if b == 0:
            src = None
            if phase == 0:
                src = ins[w].at[:, pl.ds(c0, h0 + h1)]
            cs = [copy(u, own, full, plus, *sem(0), src=src), copy(u, own, full, minus, *sem(1), src=src)]
        else:
            cs = [copy(u, block(u, phase, pm), A, plus, *sem(2)), copy(u, block(u, phase, pp), B, minus, *sem(3))]
        for c in cs: c.start()
        pending.extend(cs)
        state[(u, k)] = cs
    def arrive(u, k):
        w, g, c0, h0, h1 = U[u]
        phase, b = divmod(k, 2)
        pos = at[ORDERS[g][phase]]
        pp, pm, po = (lax.rem(pos + i, 4) for i in (1, 3, 2))
        full, A, B = (c0, h0 + h1), (c0, h0), (c0 + h0, h1)
        if b == 0:
            copy(u, block(u, phase, pm), full, me, send.at[u, phase, 0], recv.at[u, phase, 0]).wait_recv()
            copy(u, block(u, phase, pp), full, me, send.at[u, phase, 1], recv.at[u, phase, 1]).wait_recv()
        else:
            copy(u, block(u, phase, po), A, me, send.at[u, phase, 2], recv.at[u, phase, 2]).wait_recv()
            copy(u, block(u, phase, po), B, me, send.at[u, phase, 3], recv.at[u, phase, 3]).wait_recv()
    def to_sib(u, j):
        if not sib: return
        w, g, c0, h0, h1 = U[u]
        pos = at[ORDERS[g][2]]
        p = (pos, lax.rem(pos + 1, 4), lax.rem(pos + 3, 4), lax.rem(pos + 2, 4))[j]
        c = copy(u, block(u, 2, p), (c0, h0 + h1), sibling, ssend.at[u, j], srecv.at[u, j])
        c.start(); pending.append(c)
    nch = 3
    chunks = [[u for u in range(len(U)) if CHUNK[U[u][0]] == c] for c in range(nch)]
    for t in range(nch + 6):
        if t == 1:
            for c in locals_: c.wait()
        for c in range(nch):
            k = t - c
            if 0 <= k <= 6:
                for u in chunks[c]:
                    if k > 0: arrive(u, k - 1)
                    if k < 6: sub(u, k)
                    if k == 4: to_sib(u, 0)
                    if k == 5: to_sib(u, 1); to_sib(u, 2)
                    if k == 6: to_sib(u, 3)
    for c in pending: c.wait_send()
    if sib:
        for u in range(len(U)):
            w, g, c0, h0, h1 = U[u]
            pos = at[ORDERS[g][2]]
            for j, d in enumerate((0, 1, 3, 2)):
                kind = "cols" if w < 2 else "rows"
                ref = slot(outs[w], block(u, 2, lax.rem(pos + d, 4)), 1 - core, (c0, h0 + h1), kind)
                pltpu.make_async_remote_copy(src_ref=ref, dst_ref=ref, send_sem=ssend.at[u, j], recv_sem=srecv.at[u, j], device_id=sibling, device_id_type=MESH).wait_recv()

def gather(p0, p1, p2, p3, sib=True):
    nu = len(units())
    bf = jnp.bfloat16
    return pl.pallas_call(
        functools.partial(gather_kernel, sib),
        out_shape=(jax.ShapeDtypeStruct((2, 4, 4, 2, 16, 4352), bf), jax.ShapeDtypeStruct((2, 4, 4, 2, 16, 4352), bf),
                   jax.ShapeDtypeStruct((2, 4, 4, 2, 2, 32, 1088), bf), jax.ShapeDtypeStruct((2, 4, 4, 2, 2, 16, 512), bf)),
        in_specs=[pl.BlockSpec(memory_space=pl.ANY)] * 4,
        out_specs=(pl.BlockSpec(memory_space=pl.ANY),) * 4,
        scratch_shapes=[pltpu.SemaphoreType.DMA((nu, 3, 4)), pltpu.SemaphoreType.DMA((nu, 3, 4)),
                        pltpu.SemaphoreType.DMA((nu, 4)), pltpu.SemaphoreType.DMA((nu, 4)), pltpu.SemaphoreType.DMA((4,))],
        compiler_params=pltpu.CompilerParams(collective_id=0, has_side_effects=True),
    )(p0, p1, p2, p3)


def scatter_units():
    out = [(3, 0, 0, 256, 256)]
    out += [(2, 0, 0, 256, 128), (2, 1, 384, 256, 128), (2, 2, 768, 256, 128)]
    for w in (1, 0):
        out += [(w, 0, 0, 384, 384), (w, 1, 768, 384, 384), (w, 2, 1536, 384, 256)]
    return out

ROWS = (16, 16, 32, 16)
SCATTER_CHUNK = {3: 0, 2: 0, 1: 1, 0: 2}

def block_dims(order, phase):
    free = order[phase + 1:]
    dims = []
    if "z" in free: dims.append(2)
    if "x" in free: dims.append(4)
    if "y" in free: dims.append(4)
    if "z" in free: dims.append(2)
    return tuple(dims)

def part(ref, idx, cols):
    every = slice(None)
    z = idx["z"]
    zh, zl = (every, every) if z is None else (z // 2, lax.rem(z, 2))
    x = every if idx["x"] is None else idx["x"]
    y = every if idx["y"] is None else idx["y"]
    return ref.at[zh, x, y, zl, :, pl.ds(cols[0], cols[1])]

def scatter_kernel(l1a, l1b, r1, l2, r2, l3, r3, pr, o0, o1, o2, o3, *scratch):
    U = scatter_units()
    at, core = place()
    me = device(at, core)
    sibling = device(at, 1 - core)
    partner_at = {**at, "z": at["z"] + 1 - 2 * lax.rem(at["z"], 2)}
    partner, diagonal = device(partner_at, core), device(partner_at, 1 - core)
    near = {(a, s): device(moved(at, a, s), core) for a in AXES for s in (1, -1)}
    s = list(scratch)
    part_sum = s[:4]; del s[:4]
    sl1a, sl1b, sr1, sl2, sr2, sl3, sr3, spr = s[:8]; del s[:8]
    bufs = {}
    for u in range(len(U)):
        for p in range(3):
            bufs[u, p] = s[:2]; del s[:2]
    send, recv, xsend, xrecv, rsend, rrecv, lsem = s
    barrier = pltpu.get_barrier_semaphore()
    for d in list(near.values()) + [sibling, diagonal]:
        pl.semaphore_signal(barrier, inc=1, device_id=d, device_id_type=MESH)
    pl.semaphore_wait(barrier, 8)
    pending = []
    other = 1 - core
    exchange = {}
    def give(i, src, dst):
        c = pltpu.make_async_remote_copy(src_ref=src, dst_ref=dst, send_sem=xsend.at[i], recv_sem=xrecv.at[i], device_id=sibling, device_id_type=MESH)
        c.start(); pending.append(c); exchange[i] = c
    give(0, pr.at[other], spr)
    give(1, l3.at[other], sl3)
    give(2, r3, sr3)
    give(3, l2, sl2)
    give(4, r2.at[other], sr2)
    give(5, l1a, sl1a)
    give(6, l1b.at[other], sl1b)
    give(7, r1.at[other], sr1)

    def compute(w):
        f32, bf = jnp.float32, jnp.bfloat16
        P = part_sum[w]
        if w == 3:
            exchange[0].wait_recv()
            def body(i, carry):
                zh, x = i // 4, lax.rem(i, 4)
                P[zh, x] = (pr[core, zh, x].astype(f32) + spr[zh, x].astype(f32)).astype(bf)
                return carry
            lax.fori_loop(0, 8, body, 0)
            return
        need = {2: (1, 2), 1: (3, 4), 0: (5, 6, 7)}[w]
        for i in need: exchange[i].wait_recv()
        R = ROWS[w]
        step = 8 * R
        if w == 2:
            plan = [(lambda sl: l3[core, sl, :], lambda sl: sl3[sl, :], lambda c, n: r3[:, c:c + n], lambda c, n: sr3[:, c:c + n], [(0, 384), (384, 384), (768, 384)])]
        elif w == 1:
            plan = [(lambda sl: l2[sl, :], lambda sl: sl2[sl, :], lambda c, n: r2[core, :, c:c + n], lambda c, n: sr2[:, c:c + n], [(0, 768), (768, 768), (1536, 640)])]
        else:
            plan = [(lambda sl: l1a[sl, :], lambda sl: sl1a[sl, :], lambda c, n: r1[core, :, c:c + n], lambda c, n: sr1[:, c:c + n], [(0, 1088)]),
                    (lambda sl: l1b[core, sl, :], lambda sl: sl1b[sl, :], lambda c, n: r1[core, :, c:c + n], lambda c, n: sr1[:, c:c + n], [(1088, 1088)])]
        def body(i, carry):
            zh, x = i // 4, lax.rem(i, 4)
            sl = pl.ds(pl.multiple_of(i * step, step), step)
            for la, lb, ra, rb, cols in plan:
                mine, theirs = la(sl), lb(sl)
                for c, n in cols:
                    t = jnp.dot(mine, ra(c, n), preferred_element_type=f32) + jnp.dot(theirs, rb(c, n), preferred_element_type=f32)
                    t = t.astype(bf)
                    for y in range(4):
                        for zl in range(2):
                            j = (y * 2 + zl) * R
                            P[zh, x, y, zl, :, c:c + n] = t[j:j + R]
            return carry
        lax.fori_loop(0, 8, body, 0)

    def block(u, phase, pos):
        order = ORDERS[U[u][1]][::-1]
        idx = {a: at[a] for a in AXES}
        idx[order[phase]] = pos
        for a in order[phase + 1:]:
            idx[a] = None
        return idx
    def info(u, phase):
        w, g, c0, h0, h1 = U[u]
        axis = ORDERS[g][::-1][phase]
        pos = at[axis]
        pp, pm, po = (lax.rem(pos + i, 4) for i in (1, 3, 2))
        return w, (c0, h0), (c0 + h0, h1), near[axis, 1], near[axis, -1], pos, pp, pm, po
    def rc(u, phase, i, src, dst, dev):
        return pltpu.make_async_remote_copy(src_ref=src, dst_ref=dst, send_sem=send.at[u, phase, i], recv_sem=recv.at[u, phase, i], device_id=dev, device_id_type=MESH)
    def copies(u, phase):
        w, A, B, plus, minus, pos, pp, pm, po = info(u, phase)
        P = part_sum[w]
        ba, bb = bufs[u, phase]
        blk = lambda p, cols: part(P, block(u, phase, p), cols)
        return [rc(u, phase, 0, blk(po, A), ba.at[0], plus), rc(u, phase, 1, blk(po, B), bb.at[0], minus),
                rc(u, phase, 2, blk(pp, B), bb.at[1], plus), rc(u, phase, 3, blk(pm, A), ba.at[1], minus),
                rc(u, phase, 4, blk(pp, A), ba.at[2], plus), rc(u, phase, 5, blk(pm, B), bb.at[2], minus)]
    live = {}
    def step_a(u, phase):
        cs = live[u, phase] = copies(u, phase)
        for c in cs[:4]: c.start()
        pending.extend(cs)
    def add(ref, *others):
        t = ref[...].astype(jnp.float32)
        for o in others: t = t + o[...].astype(jnp.float32)
        ref[...] = t.astype(jnp.bfloat16)
    def step_b(u, phase):
        w, A, B, plus, minus, pos, pp, pm, po = info(u, phase)
        cs = live[u, phase]
        P = part_sum[w]; ba, bb = bufs[u, phase]
        cs[0].wait_recv()
        add(part(P, block(u, phase, pp), A), ba.at[0])
        cs[4].start()
        cs[1].wait_recv()
        add(part(P, block(u, phase, pm), B), bb.at[0])
        cs[5].start()
    def step_c(u, phase):
        w, A, B, plus, minus, pos, pp, pm, po = info(u, phase)
        cs = live[u, phase]
        P = part_sum[w]; ba, bb = bufs[u, phase]
        cs[3].wait_recv(); cs[4].wait_recv()
        add(part(P, block(u, phase, pos), A), ba.at[1], ba.at[2])
        cs[2].wait_recv(); cs[5].wait_recv()
        add(part(P, block(u, phase, pos), B), bb.at[1], bb.at[2])
    outs = (o0, o1, o2, o3)
    def out_part(w, zl, c, cols):
        if w < 2:
            return outs[w].at[zl, :, pl.ds(pl.multiple_of(c * 2176 + cols[0], 128), cols[1])]
        return outs[w].at[zl, c, :, pl.ds(cols[0], cols[1])]
    reps = []
    def share(u):
        w, g, c0, h0, h1 = U[u]
        src = part(part_sum[w], at, (c0, h0 + h1))
        dst = out_part(w, lax.rem(at["z"], 2), core, (c0, h0 + h1))
        c = pltpu.make_async_copy(src, dst, lsem.at[u]); c.start(); reps.append(c)
        for i, dev in enumerate((sibling, partner, diagonal)):
            c = pltpu.make_async_remote_copy(src_ref=src, dst_ref=dst, send_sem=rsend.at[u, i], recv_sem=rrecv.at[u, i], device_id=dev, device_id_type=MESH)
            c.start(); pending.append(c)
    def share_wait(u):
        w, g, c0, h0, h1 = U[u]
        zl = lax.rem(at["z"], 2)
        src = part(part_sum[w], at, (c0, h0 + h1))
        for i, (z, c) in enumerate(((zl, 1 - core), (1 - zl, core), (1 - zl, 1 - core))):
            pltpu.make_async_remote_copy(src_ref=src, dst_ref=out_part(w, z, c, (c0, h0 + h1)), send_sem=rsend.at[u, i], recv_sem=rrecv.at[u, i], device_id=me, device_id_type=MESH).wait_recv()
    chunks = [[u for u in range(len(U)) if SCATTER_CHUNK[U[u][0]] == c] for c in range(3)]
    for t in range(3 + 7):
        for c in range(3):
            k = t - c
            if k < 0 or k > 7: continue
            if k == 0:
                for w in sorted({U[u][0] for u in chunks[c]}, reverse=True): compute(w)
            for u in chunks[c]:
                if k == 0: step_a(u, 0)
                elif k in (1, 3, 5): step_b(u, k // 2)
                elif k in (2, 4): step_c(u, k // 2 - 1); step_a(u, k // 2)
                elif k == 6: step_c(u, 2); share(u)
                elif k == 7: share_wait(u)
    for c in reps: c.wait()
    for c in pending: c.wait_send()

def scatter(*ops):
    U = scatter_units()
    bf = jnp.bfloat16
    V = pltpu.VMEM
    scratch = [V((2, 4, 4, 2, 16, 2176), bf), V((2, 4, 4, 2, 16, 2176), bf), V((2, 4, 4, 2, 32, 1152), bf), V((2, 4, 4, 2, 16, 512), bf)]
    scratch += [V((1024, 160), bf), V((1024, 160), bf), V((160, 2176), bf), V((1024, 160), bf), V((160, 2176), bf), V((2048, 160), bf), V((160, 1152), bf), V((2, 4, 4, 2, 16, 512), bf)]
    for w, g, c0, h0, h1 in U:
        for p in range(3):
            dims = block_dims(ORDERS[g][::-1], p)
            scratch += [V((3,) + dims + (ROWS[w], h0), bf), V((3,) + dims + (ROWS[w], h1), bf)]
    n = len(U)
    D = pltpu.SemaphoreType.DMA
    scratch += [D((n, 3, 6)), D((n, 3, 6)), D((8,)), D((8,)), D((n, 3)), D((n, 3)), D((n,))]
    return pl.pallas_call(
        scatter_kernel,
        out_shape=(jax.ShapeDtypeStruct((2, 16, 4352), bf), jax.ShapeDtypeStruct((2, 16, 4352), bf),
                   jax.ShapeDtypeStruct((2, 2, 32, 1152), bf), jax.ShapeDtypeStruct((2, 2, 16, 512), bf)),
        in_specs=[pl.BlockSpec(memory_space=pltpu.VMEM)] * 8,
        out_specs=(pl.BlockSpec(memory_space=pl.ANY),) * 4,
        scratch_shapes=scratch,
        compiler_params=pltpu.CompilerParams(collective_id=1, has_side_effects=True, vmem_limit_bytes=60 * 2**20),
    )(*ops)

HEADS = 17
HEAD_DIM = 64
WIDTH = 1088
HIDDEN = 4352
epsilon = 1e-05
excluded = -1000000000.0
F32, BF16 = jnp.float32, jnp.bfloat16


def dealt():
    natural = lax.broadcasted_iota(jnp.int32, (WIDTH, WIDTH), 0)
    place_ = lax.broadcasted_iota(jnp.int32, (WIDTH, WIDTH), 1)
    block, row = natural // 34, natural % 34
    target = jnp.where(row < 32, block * 32 + row, 1024 + block * 2 + row - 32)
    return (target == place_).astype(BF16)


def dot(a, b, dims=((1,), (0,))):
    return lax.dot_general(a, b, (dims, ((), ())), preferred_element_type=F32)


def layer_norm(values, norm_gain, norm_shift):
    average = jnp.mean(values, axis=-1, keepdims=True)
    centered = values - average
    variance = jnp.mean(centered * centered, axis=-1, keepdims=True)
    return centered * lax.rsqrt(variance + epsilon) * norm_gain + norm_shift


def gelu_tanh(values):
    return jax.nn.gelu(values, approximate=True)


def causal_segments(seq_lengths, count):
    ends = jnp.cumsum(seq_lengths)
    position = jnp.arange(count, dtype=jnp.int32)
    segment = jnp.sum((position[:, None] >= ends[None, :]).astype(jnp.int32), axis=1)
    return (segment[:, None] == segment[None, :]) & (position[:, None] >= position[None, :])


def head_split(rows):
    return rows.reshape(rows.shape[0], HEADS, HEAD_DIM)


def column_sum(rows):
    return jnp.sum(rows.astype(F32), axis=0)


def own_pieces(q, core, perm, vectors, qkv_weight, out_weight, up_weight, down_weight):
    stacked = jnp.concatenate([out_weight, up_weight.reshape(136, WIDTH), down_weight], axis=0)
    stacked = dot(stacked, perm).astype(BF16)
    out_d, up_d, down_d = stacked[:34], stacked[34:170].reshape(34, 4, WIDTH), stacked[170:].reshape(4, 34, WIDTH)
    up_d = jnp.concatenate([up_d[:, :, :1024].reshape(34, 4096), up_d[:, :, 1024:].reshape(34, 256)], axis=1)
    first = jnp.concatenate([qkv_weight, out_d], axis=1)
    zl = q // 2
    p0 = lax.dynamic_slice(first, (zl * 16, core * 2176), (16, 2176))
    p1 = lax.dynamic_slice(up_d, (zl * 16, core * 2176), (16, 2176))
    p2 = lax.dynamic_slice(down_d, (q, 0, 0), (1, 32, WIDTH))[0]
    bias = jnp.concatenate(vectors + [jnp.zeros((104,), BF16)]).reshape(1, 512)
    rest = jnp.concatenate(
        [jnp.concatenate([first[32:], up_d[32:]], axis=1).reshape(34, 512), down_d[:, 32:].reshape(17, 512), bias, jnp.zeros((12, 512), BF16)],
        axis=0,
    )
    p3 = lax.dynamic_slice(rest, (q * 16, 0), (16, 512))
    return p0, p1, p2, p3


def dealt_vector(blocks):
    return jnp.concatenate([blocks[:, :32].reshape(-1), blocks[:, 32:].reshape(-1)])


def back_vector(values, blocks):
    return jnp.concatenate([values[: 32 * blocks].reshape(blocks, 32), values[32 * blocks :].reshape(blocks, 2)], axis=1)


def body(tokens, lengths, cotangent, attn_gain, attn_shift, qkv_weight, query_bias, value_bias, out_weight, out_bias, mlp_gain, mlp_shift, up_weight, up_bias, down_weight, down_bias):
    rank = lax.axis_index("rep")
    core = rank % 2
    perm = dealt()
    count = tokens.shape[0]
    vectors = [attn_gain, attn_shift, query_bias, value_bias, out_bias, mlp_gain, mlp_shift, down_bias, up_bias]
    g0, g1, g2, g3 = gather(*own_pieces(rank, core, perm, vectors, qkv_weight, out_weight, up_weight, down_weight))
    W1, W2, W3 = g0.reshape(1024, HIDDEN), g1.reshape(1024, HIDDEN), g2.reshape(4096, WIDTH)
    rest = g3.reshape(32, 64, 512)
    wide = rest[:, :34].reshape(64, 8704)
    V1, V2 = wide[:, :HIDDEN], wide[:, HIDDEN:]
    V3 = rest[:, 34:51].reshape(256, WIDTH)
    small = rest[:, 51, :408].astype(F32)
    gain_first, shift_first, out_shift, gain_second, shift_second, down_shift = (dealt_vector(small[:, 34 * i : 34 * i + 34]) for i in (0, 1, 4, 5, 6, 7))
    query_shift, value_shift = (small[:, 34 * i : 34 * i + 34].reshape(-1) for i in (2, 3))
    up_shift = dealt_vector(small[:, 272:408].reshape(128, 34))

    def up_from(x, main, left):
        return dot(x[:, : main.shape[0]], main) + dot(x[:, main.shape[0] :], left)

    def down_to(g, main, left):
        return jnp.concatenate([dot(g, main, ((1,), (1,))), dot(g, left, ((1,), (1,)))], axis=1)

    allowed = causal_segments(lengths[0], count)
    stream = dot(tokens, perm)
    upstream = dot(cotangent, perm)
    out_low = upstream.astype(BF16)
    normed_first = layer_norm(stream, gain_first, shift_first).astype(BF16)
    projected = up_from(normed_first, W1[:, :3328], V1[:, :3328])
    query = (projected[:, :WIDTH] + query_shift).astype(BF16)
    key = projected[:, WIDTH : 2 * WIDTH].astype(BF16)
    value = (projected[:, 2 * WIDTH : 3264] + value_shift).astype(BF16)
    query_heads, key_heads, value_heads = head_split(query), head_split(key), head_split(value)
    scores = jnp.einsum("qhd,khd->hqk", query_heads, key_heads, preferred_element_type=F32)
    scores = jnp.where(allowed[None], scores * HEAD_DIM ** (-0.5), excluded)
    largest = jnp.max(scores, axis=-1, keepdims=True)
    log_total = largest + jnp.log(jnp.sum(jnp.exp(scores - largest), axis=-1, keepdims=True))
    probs = jnp.exp(scores - log_total)
    probs_low = probs.astype(BF16)
    mixed = jnp.einsum("hqk,khd->qhd", probs_low, value_heads, preferred_element_type=F32)
    attended = dot(mixed.reshape(count, WIDTH).astype(BF16), perm).astype(BF16)
    resid = stream + up_from(attended, W1[:, 3200:], V1[:, 3200:])[:, 64:] + out_shift
    normed_second = layer_norm(resid, gain_second, shift_second).astype(BF16)
    hidden = up_from(normed_second, W2, V2) + up_shift
    activated = gelu_tanh(hidden).astype(BF16)
    layer_out = resid + up_from(activated, W3, V3) + down_shift
    activated_grad = down_to(out_low, W3, V3)
    unused, gelu_back = jax.vjp(gelu_tanh, hidden)
    hidden_grad = gelu_back(activated_grad)[0].astype(BF16)
    normed_grad = down_to(hidden_grad, W2, V2)
    unused, norm_back = jax.vjp(layer_norm, resid, gain_second, shift_second)
    resid_part, mlp_gain_part, mlp_shift_part = norm_back(normed_grad)
    resid_grad = upstream + resid_part
    branch_low = resid_grad.astype(BF16)
    attended_grad = down_to(jnp.pad(branch_low, ((0, 0), (64, 0))), W1[:, 3200:], V1[:, 3200:]).astype(BF16)
    grad_heads = head_split(dot(attended_grad, perm, ((1,), (1,))).astype(BF16))
    value_grad = jnp.einsum("hqk,qhd->khd", probs_low, grad_heads, preferred_element_type=F32).astype(BF16).reshape(count, WIDTH)
    prob_grad = jnp.einsum("qhd,khd->hqk", grad_heads, value_heads, preferred_element_type=F32)
    score_grad = (probs * (prob_grad - jnp.sum(probs * prob_grad, axis=-1, keepdims=True))).astype(BF16)
    scale = HEAD_DIM ** (-0.5)
    query_grad = (jnp.einsum("hqk,khd->qhd", score_grad, key_heads, preferred_element_type=F32) * scale).astype(BF16).reshape(count, WIDTH)
    key_grad = (jnp.einsum("hqk,qhd->khd", score_grad, query_heads, preferred_element_type=F32) * scale).astype(BF16).reshape(count, WIDTH)
    qkv_grad = jnp.concatenate([query_grad, key_grad, value_grad, jnp.zeros((count, 64), BF16)], axis=1)
    normed_grad = down_to(qkv_grad, W1[:, :3328], V1[:, :3328])
    unused, norm_back = jax.vjp(layer_norm, stream, gain_first, shift_first)
    input_part, attn_gain_part, attn_shift_part = norm_back(normed_grad)
    input_grad = resid_grad + input_part
    l1a = normed_first[:, :1024].T
    l1b = jnp.stack([l1a, attended[:, :1024].T])
    r1 = jnp.stack([qkv_grad[:, :2176], jnp.concatenate([value_grad, branch_low], axis=1)])
    l2 = normed_second[:, :1024].T
    r2 = jnp.stack([hidden_grad[:, :2176], hidden_grad[:, 2176:]])
    l3 = activated[:, :4096].T.reshape(32, 2, 2, 32, count)
    l3 = jnp.stack([l3[:, :, 0].reshape(2048, count), l3[:, :, 1].reshape(2048, count)])
    r3 = jnp.pad(out_low, ((0, 0), (0, 64)))
    tdot = lambda a, b: dot(a, b, ((0,), (0,)))
    left1 = jnp.concatenate(
        [tdot(normed_first[:, 1024:], qkv_grad[:, :3264]), tdot(attended[:, 1024:], branch_low), tdot(normed_second[:, 1024:], hidden_grad)], axis=1
    ).astype(BF16)
    left3 = tdot(activated[:, 4096:], out_low).astype(BF16)
    sums = [back_vector(v, 32) for v in (attn_gain_part, attn_shift_part)]
    sums += [column_sum(query_grad).reshape(32, 34), column_sum(value_grad).reshape(32, 34)]
    sums += [back_vector(v, 32) for v in (column_sum(branch_low), mlp_gain_part, mlp_shift_part, column_sum(out_low))]
    sums += [back_vector(column_sum(hidden_grad), 128).reshape(32, 136), jnp.zeros((32, 104), F32)]
    left = jnp.concatenate(
        [left1.reshape(32, 34, 512), left3.reshape(32, 17, 512), jnp.concatenate(sums, axis=1).astype(BF16).reshape(32, 1, 512), jnp.zeros((32, 12, 512), BF16)],
        axis=1,
    )
    pr = jnp.moveaxis(left.reshape(2, 4, 4, 2, 2, 16, 512), 4, 0)
    s0, s1, s2, s3 = scatter(l1a, l1b, r1, l2, r2, l3, r3, pr)
    left = s3.reshape(64, 512)
    wide = left[:34].reshape(2, 8704)
    first = jnp.concatenate([s0.reshape(32, HIDDEN), wide[:, :HIDDEN]], axis=0)
    up_d = jnp.concatenate([s1.reshape(32, HIDDEN), wide[:, HIDDEN:]], axis=0)
    up_d = jnp.concatenate([up_d[:, :4096].reshape(34, 4, 1024), up_d[:, 4096:].reshape(34, 4, 64)], axis=2)
    down_d = jnp.concatenate([s2.reshape(4, 32, 1152)[:, :, :WIDTH], left[34:51].reshape(4, 2, WIDTH)], axis=1)
    stacked = jnp.concatenate([first[:, 3264:], up_d.reshape(136, WIDTH), down_d.reshape(136, WIDTH)], axis=0)
    stacked = dot(stacked, perm, ((1,), (1,)))
    small = left[51].astype(F32)
    v = [small[34 * i : 34 * i + 34] for i in range(8)] + [small[272:408]]
    natural_out = dot(layer_out.astype(BF16), perm, ((1,), (1,))).astype(BF16)
    natural_grad = lax.dot_general(input_grad, perm.astype(F32), (((1,), (1,)), ((), ())), precision=lax.Precision.HIGHEST, preferred_element_type=F32)
    return (
        natural_out,
        natural_grad,
        v[0],
        v[1],
        first[:, :3264].astype(F32),
        v[2],
        v[3],
        stacked[:34],
        v[4],
        v[5],
        v[6],
        stacked[34:170].reshape(34, HIDDEN),
        v[8],
        stacked[170:],
        v[7],
    )


def solution(mesh):
    tokens_spec, matrix, vector = P(("fsdp", "rep"), None), P("fsdp", None), P("fsdp")
    return jax.shard_map(
        body,
        mesh=mesh,
        in_specs=(tokens_spec, tokens_spec, tokens_spec, vector, vector, matrix, vector, vector, matrix, vector, vector, vector, matrix, vector, matrix, vector),
        out_specs=(tokens_spec, tokens_spec, vector, vector, matrix, vector, vector, matrix, vector, vector, vector, matrix, vector, matrix, vector),
        check_vma=False,
    )
```

```python
import jax, jax.numpy as jnp
from jax import lax
from jax.experimental import pallas as pl
from jax.experimental.pallas import tpu as pltpu
from jax.sharding import PartitionSpec as P

MESH = pl.DeviceIdType.MESH
F32, BF16 = jnp.float32, jnp.bfloat16
AXES = "xyz"
ORDERS = ("xyz", "yzx", "zxy")
TOK = 160
WIDE = 1152
REAL = 1088
FF = 4352
epsilon = 1e-05
excluded = -1000000000.0
PER_STEP = 3
ROOT = 0.7978845608028654


def place():
    f = lax.axis_index("fsdp")
    r = lax.axis_index("rep")
    return dict(x=(f // 4) % 4, y=f % 4, z=(f // 16) * 2 + r // 2), r % 2


def device(at, core):
    z = at["z"]
    return ((z // 2) * 16 + at["x"] * 4 + at["y"], (z % 2) * 2 + core)


def moved(at, axis, step):
    return {**at, axis: lax.rem(at[axis] + step + 4, 4)}


def meet(devices):
    barrier = pltpu.get_barrier_semaphore()
    for d in devices:
        pl.semaphore_signal(barrier, inc=1, device_id=d, device_id_type=MESH)
    pl.semaphore_wait(barrier, len(devices))


def dot(a, b):
    return jnp.dot(a, b, preferred_element_type=F32)


def dot_nt(a, b):
    return lax.dot_general(a, b, (((1,), (1,)), ((), ())), preferred_element_type=F32)


def iota(shape, dim):
    return lax.broadcasted_iota(jnp.int32, shape, dim)


def eye(n):
    return jnp.where(iota((n, n), 0) == iota((n, n), 1), 1.0, 0.0).astype(BF16)


def dealt_pick():
    r, c = iota((128, WIDE), 0), iota((128, WIDE), 1)
    want = jnp.where(c < 1024, c & 31, jnp.where(c < REAL, 32 + ((c - 1024) >> 5), -1))
    s, c = iota((32, WIDE), 0), iota((32, WIDE), 1)
    owner = jnp.where(c < 1024, c >> 5, c & 31)
    return jnp.where(r == want, 1.0, 0.0).astype(BF16), jnp.where(s == owner, 1.0, 0.0)


def hidden_pick(k):
    r, c = iota((128, FF), 0), iota((128, FF), 1)
    want = jnp.where(c < 4096, c & 31, 32 + (((c - 4096) >> 5) & 1))
    s, c = iota((32, FF), 0), iota((32, FF), 1)
    d = c - 4096
    owner = jnp.where(c < 4096, c >> 5, 4 * (d & 31) + (d >> 6))
    return jnp.where(r == want, 1.0, 0.0).astype(BF16), jnp.where(4 * s + k == owner, 1.0, 0.0)


def centred(values):
    valid = iota((1, WIDE), 1) < REAL
    average = jnp.sum(values, axis=-1, keepdims=True) * (1.0 / REAL)
    c = jnp.where(valid, values - average, 0.0)
    r = lax.rsqrt(jnp.sum(c * c, axis=-1, keepdims=True) * (1.0 / REAL) + epsilon)
    return c * r, r


def gather_chunks():
    whole = [
        [(3, 0, 0, 16, 0, 256, 256)],
        [(0, g, 0, 16, 768 * g, 384, 384) for g in range(3)],
        [(1, 0, 0, 16, 0, 384, 384), (1, 1, 0, 16, 768, 384, 384), (1, 2, 0, 16, 1536, 384, 256)],
        [(2, g, 0, 32, 384 * g, 256, 128) for g in range(3)],
    ]
    parts = [
        [(3, 0, 0, 16, 0, 256, 256)],
        [(0, g, 0, 16, 768 * g, 256, 128) for g in range(3)],
        [(0, g, 0, 16, 768 * g + 384, 256, 128) for g in range(3)],
        [(1, g, 0, 16, 768 * g, 256, 128) for g in range(3)],
        [(1, 0, 0, 16, 384, 256, 128), (1, 1, 0, 16, 1152, 256, 128), (1, 2, 0, 16, 1920, 128, 128)],
        [(2, g, 0, 16, 384 * g, 256, 128) for g in range(3)],
        [(2, g, 16, 16, 384 * g, 256, 128) for g in range(3)],
    ]
    return whole, parts


HALF = (2304, 2176)


def slot(ref, w, idx, core, rows, cols):
    z = idx["z"]
    every = slice(None)
    zh, zl = (every, every) if z is None else (z // 2, lax.rem(z, 2))
    x = every if idx["x"] is None else idx["x"]
    y = every if idx["y"] is None else idx["y"]
    if w < 2:
        return ref.at[zh, x, y, zl, :, pl.ds(pl.multiple_of(core * HALF[w] + cols[0], 128), cols[1])]
    return ref.at[zh, x, y, zl, core, pl.ds(rows[0], rows[1]), pl.ds(cols[0], cols[1])]


def forward_kernel(
    p0, p1, p2, p3, tokens, cot, perm, bias,
    g0, g1, g2, g3, v1, v2, vecs, lt, nst, actt, qkv, resid, ns, hg, out,
    w1, w2, w3, rest, unpacked, v3, upb, nf, att, attd, act, gp,
    send, recv, ssend, srecv, lsem, wsem,
):
    at, core = place()
    me = device(at, core)
    sibling = device(at, 1 - core)
    near = {(a, s): device(moved(at, a, s), core) for a in AXES for s in (1, -1)}
    meet(list(near.values()) + [sibling])
    ins, outs = (p0, p1, p2, p3), (g0, g1, g2, g3)
    whole, parts = gather_chunks()
    U = [u for c in whole + parts for u in c]
    ids, n = [], 0
    for c in whole + parts:
        ids.append(list(range(n, n + len(c))))
        n += len(c)
    whole_ids, part_ids = ids[: len(whole)], ids[len(whole) :]
    pending = []

    def block(u, phase, pos):
        order = ORDERS[U[u][1]]
        idx = dict(at)
        for a in order[:phase]:
            idx[a] = None
        idx[order[phase]] = pos
        return idx

    def copy(u, idx, cols, dev, s, r, src=None, c=None):
        w, g, r0, nr = U[u][:4]
        ref = slot(outs[w], w, idx, core if c is None else c, (r0, nr), cols)
        return pltpu.make_async_remote_copy(
            src_ref=ref if src is None else src, dst_ref=ref, send_sem=s, recv_sem=r, device_id=dev, device_id_type=MESH
        )

    def spots(u, phase):
        w, g, r0, nr, c0, h0, h1 = U[u]
        axis = ORDERS[g][phase]
        pos = at[axis]
        return axis, pos, [lax.rem(pos + i, 4) for i in (1, 3, 2)], (c0, h0 + h1), (c0, h0), (c0 + h0, h1)

    def go(u, k):
        w, g, r0, nr, c0, h0, h1 = U[u]
        phase, b = divmod(k, 2)
        axis, pos, (pp, pm, po), full, A, B = spots(u, phase)
        plus, minus = near[axis, 1], near[axis, -1]
        sem = lambda i: (send.at[u, phase, i], recv.at[u, phase, i])
        if b == 0:
            src = ins[w].at[pl.ds(r0, nr), pl.ds(c0, h0 + h1)] if phase == 0 else None
            own = block(u, phase, pos)
            cs = [copy(u, own, full, plus, *sem(0), src=src), copy(u, own, full, minus, *sem(1), src=src)]
        else:
            cs = [copy(u, block(u, phase, pm), A, plus, *sem(2)), copy(u, block(u, phase, pp), B, minus, *sem(3))]
        for c in cs:
            c.start()
        pending.extend(cs)

    def arrive(u, k):
        phase, b = divmod(k, 2)
        axis, pos, (pp, pm, po), full, A, B = spots(u, phase)
        pairs = ((pm, full, 0), (pp, full, 1)) if b == 0 else ((po, A, 2), (po, B, 3))
        for p, cols, i in pairs:
            copy(u, block(u, phase, p), cols, me, send.at[u, phase, i], recv.at[u, phase, i]).wait_recv()

    def across(u, j):
        axis, pos, others, full, A, B = spots(u, 2)
        p = ([pos] + others)[j]
        c = copy(u, block(u, 2, p), full, sibling, ssend.at[u, j], srecv.at[u, j])
        c.start()
        pending.append(c)

    def arrive_across(u):
        axis, pos, others, full, A, B = spots(u, 2)
        for j, p in enumerate([pos] + others):
            copy(u, block(u, 2, p), full, me, ssend.at[u, j], srecv.at[u, j], c=1 - core).wait_recv()

    own_copies = []
    for w in range(4):
        cols = (0, (2304, 2176, WIDE, 512)[w])
        rows = (0, (16, 16, 32, 16)[w])
        c = pltpu.make_async_copy(ins[w], slot(outs[w], w, at, core, rows, cols), lsem.at[w])
        c.start()
        own_copies.append(c)

    def early(c, k):
        def run():
            for u in whole_ids[c]:
                if k > 0:
                    arrive(u, k - 1)
                if k < 4:
                    go(u, k)
        return run

    def third(c):
        def run():
            for u in part_ids[c]:
                go(u, 4)
            for u in part_ids[c]:
                across(u, 0)
        return run

    def onward(c):
        def run():
            for u in part_ids[c]:
                arrive(u, 4)
                go(u, 5)
            for u in part_ids[c]:
                across(u, 1)
                across(u, 2)
        return run

    def last(c):
        def run():
            for u in part_ids[c]:
                arrive(u, 5)
                across(u, 3)
        return run

    loads = {}

    def load(name, src, dst, i):
        loads[name] = pltpu.make_async_copy(src, dst, wsem.at[i])
        loads[name].start()

    def landed(c):
        for u in part_ids[c]:
            arrive_across(u)

    def weight(ref, lo, n):
        return ref[:, :, :, :, :, lo : lo + n].reshape(1024, n)

    def row(i):
        return vecs[i : i + 1, :]

    def stage_rest():
        landed(0)
        load("rest", g3, rest, 3)
        loads["rest"].wait()
        for q in range(4):
            for t in range(4):
                piece = rest[:, :, :, q // 2, q % 2, :, 128 * t : 128 * t + 128].astype(F32)
                unpacked[t, q] = piece.reshape(512, 128)

    def gathered_row(i, t):
        return unpacked[t, i // 16, pl.ds(i % 16, 32, stride=16), :]

    def stage_vectors():
        pick, own = dealt_pick()
        rows = []
        for i in range(8):
            b = gathered_row(60 + i // 4, i % 4).astype(BF16)
            rows.append(jnp.sum(own * dot(b, pick), axis=0, keepdims=True))
        all_rows = jnp.concatenate(rows, axis=0)
        natural = dot_nt(all_rows.astype(BF16), perm[...])
        vecs[...] = jnp.concatenate([all_rows[:2], natural[2:4], all_rows[4:]], axis=0)

    def stage_units(k):
        def run():
            pick, own = hidden_pick(k)
            b = gathered_row(62, k).astype(BF16)
            t = jnp.sum(own * dot(b, pick), axis=0, keepdims=True)
            upb[...] = t if k == 0 else upb[...] + t
        return run

    def stage_left(w):
        def run():
            if w < 2:
                dst = (v1, v2)[w]
                for r in range(2):
                    for j in range(9):
                        for t in range(4):
                            lane = 512 * j + 128 * t
                            if lane < dst.shape[1]:
                                dst[32 * r : 32 * r + 32, lane : lane + 128] = gathered_row(18 * w + 9 * r + j, t).astype(BF16)
                dst[64:, :] = jnp.zeros((64, dst.shape[1]), BF16)
            else:
                for b in range(8):
                    for j in range(3):
                        for t in range(4):
                            lane = 512 * j + 128 * t
                            if lane < WIDE:
                                v3[32 * b : 32 * b + 32, lane : lane + 128] = gathered_row(36 + 3 * b + j, t).astype(BF16)
        return run

    def flipped(ref):
        parts = []
        for c in range(0, WIDE, 256):
            n = min(256, WIDE - c)
            parts.append((c, n, dot_nt(eye(n), ref[:, c : c + n]).astype(BF16)))
        return parts

    def stage_norm():
        xhat, r = centred(tokens[...].astype(F32))
        nf[...] = (xhat * row(0) + row(1)).astype(BF16)
        for c, n, t in flipped(nf):
            lt[0, c : c + n, :] = t

    def stage_load1():
        landed(1)
        landed(2)
        load("w1", g0, w1, 0)

    def stage_qkv(i):
        def run():
            if i == 0:
                loads["w1"].wait()
            for c in (0, 384, 768):
                lo = WIDE * i + c
                t = dot(nf[:, :1024], weight(w1, lo, 384)) + dot(nf[:, 1024:], v1[:, lo : lo + 384])
                if i != 1:
                    t = t + vecs[2 + i // 2 : 3 + i // 2, c : c + 384]
                qkv[i, :, c : c + 384] = t.astype(BF16)
        return run

    def stage_attention(pair):
        def run():
            lanes = pl.ds(128 * pair, 128)
            q, k, v = qkv[0, :, lanes], qkv[1, :, lanes], qkv[2, :, lanes]
            low_half = iota((1, 128), 1) < 64
            total = jnp.zeros((TOK, 128), F32)
            for half in range(2):
                mask = low_half if half == 0 else jnp.logical_not(low_half)
                pick = lambda t: jnp.where(mask, t, jnp.zeros_like(t))
                s = dot_nt(q, pick(k)) * 0.125 + bias[...]
                e = jnp.exp(s - jnp.max(s, axis=-1, keepdims=True))
                p = e / jnp.sum(e, axis=-1, keepdims=True)
                total = total + dot(p.astype(BF16), pick(v))
            att[:, lanes] = total.astype(BF16)
        return run

    def stage_out():
        attd[...] = dot(att[...], perm[...]).astype(BF16)
        for c in (0, 384, 768):
            lo = 3 * WIDE + c
            t = dot(attd[:, :1024], weight(w1, lo, 384)) + dot(attd[:, 1024:], v1[:, lo : lo + 384])
            resid[:, c : c + 384] = tokens[:, c : c + 384].astype(F32) + t + vecs[4:5, c : c + 384]
        for c, n, t in flipped(attd):
            lt[1, c : c + n, :] = t

    def stage_norm2():
        xhat, r = centred(resid[...])
        ns[...] = (xhat * row(5) + row(6)).astype(BF16)
        for c, n, t in flipped(ns):
            nst[c : c + n, :] = t

    def stage_load2():
        landed(3)
        landed(4)
        load("w2", g1, w2, 1)

    def stage_up(half, c, n):
        def run():
            if half == 0 and c == 0:
                loads["w2"].wait()
            lo = 2176 * half + c
            u = dot(ns[:, :1024], weight(w2, lo, n)) + dot(ns[:, 1024:], v2[:, lo : lo + n]) + upb[:, lo : lo + n]
            t = jnp.tanh(ROOT * (u + 0.044715 * u * u * u))
            a = (0.5 * u * (1.0 + t)).astype(BF16)
            act[:, lo : lo + n] = a
            gp[:, lo : lo + n] = 0.5 * (1.0 + t) + 0.5 * u * (1.0 - t * t) * (ROOT * (1.0 + 3 * 0.044715 * u * u))
            for j in range(0, n, 128):
                f = lo + j
                flip = dot_nt(eye(128), a[:, j : j + 128]).astype(BF16)
                if f < 4096:
                    actt[f // 128] = flip.reshape(2, 2, 32, TOK)
                else:
                    actt[f // 128] = flip.reshape(2, 2, 32, TOK)
        return run

    def stage_load3(i):
        def run():
            landed(5 + i)
            r = pl.ds(16 * i, 16)
            load(f"w3{i}", g2.at[:, :, :, :, :, r, :], w3.at[:, :, :, :, :, r, :], 2 + 2 * i)
        return run

    def stage_down(c):
        def run():
            if c == 0:
                loads["w30"].wait()
                loads["w31"].wait()
            t = dot(act[:, :4096], w3[:, :, :, :, :, :, c : c + 384].reshape(4096, 384))
            t = t + dot(act[:, 4096:], v3[:, c : c + 384])
            attd[:, c : c + 384] = (resid[:, c : c + 384] + t + vecs[7:8, c : c + 384]).astype(BF16)
        return run

    def stage_result():
        out[...] = dot_nt(attd[...], perm[...]).astype(BF16)

    def stage_hidden(zh, x):
        def run():
            f = (zh * 4 + x) * 512
            d = dot_nt(cot[...], w3[zh, x].reshape(512, WIDE))
            g = (d * gp[:, f : f + 512]).astype(BF16)
            put_hidden(f, 512, g)
        return run

    def put_hidden(f, n, g):
        if f + n <= 2176:
            hg[0, :, f : f + n] = g
        elif f >= 2176:
            hg[1, :, f - 2176 : f - 2176 + n] = g
        else:
            m = 2176 - f
            hg[0, :, f:2176] = g[:, :m]
            hg[1, :, : n - m] = g[:, m:]

    def stage_hidden_left():
        d = dot_nt(cot[...], v3[...])
        put_hidden(4096, 256, (d * gp[:, 4096:]).astype(BF16))

    ups = [stage_up(h, c, n) for h in range(2) for c, n in ((0, 512), (512, 512), (1024, 512), (1536, 640))]
    lefts = [stage_left(w) for w in range(3)]
    work = {
        0: [stage_rest, stage_vectors] + [stage_units(k) for k in range(4)] + [stage_norm] + lefts,
        2: [stage_load1] + [stage_qkv(i) for i in range(3)] + [stage_attention(i) for i in range(9)] + [stage_out, stage_norm2],
        4: [stage_load2] + ups,
        5: [stage_load3(0)],
        6: [stage_load3(1)] + [stage_down(c) for c in (0, 384, 768)] + [stage_result] + [stage_hidden(zh, x) for zh in range(2) for x in range(4)] + [stage_hidden_left],
    }
    queue = []

    def compute(n):
        for _ in range(min(n, len(queue))):
            queue.pop(0)()

    for k in range(4):
        for c in range(4):
            early(c, k)()
        if k == 0:
            for c in own_copies:
                c.wait()
    script = [("e", 0), ("t", 0), ("e", 1), ("t", 1), ("t", 2), ("o", 0), ("e", 2), ("t", 3), ("t", 4), ("l", 0), ("o", 1)]
    script += [("e", 3), ("t", 5), ("t", 6), ("o", 2), ("l", 1), ("o", 3), ("l", 2), ("o", 4), ("l", 3), ("o", 5), ("l", 4), ("o", 6), ("l", 5), ("l", 6)]
    waiting = []
    for kind, c in script:
        if kind == "e":
            early(c, 4)()
        else:
            {"t": third, "o": onward, "l": last}[kind](c)()
        for w in waiting:
            queue.extend(work.get(w, []))
        waiting = [c] if kind == "l" else []
        if kind != "t":
            compute(PER_STEP)
    for w in waiting:
        queue.extend(work.get(w, []))
    compute(len(queue))
    for c in pending:
        c.wait_send()


def forward_call(p0, p1, p2, p3, tokens, cot, perm, bias):
    n = sum(len(c) for group in gather_chunks() for c in group)
    D, V = pltpu.SemaphoreType.DMA, pltpu.VMEM
    here, vm = pl.BlockSpec(memory_space=pl.ANY), pl.BlockSpec(memory_space=pltpu.VMEM)
    S = jax.ShapeDtypeStruct
    outs = [
        (S((2, 4, 4, 2, 16, 4608), BF16), here), (S((2, 4, 4, 2, 16, 4352), BF16), here),
        (S((2, 4, 4, 2, 2, 32, WIDE), BF16), here), (S((2, 4, 4, 2, 2, 16, 512), BF16), here),
        (S((128, 4608), BF16), vm), (S((128, FF), BF16), vm), (S((8, WIDE), F32), vm),
        (S((2, WIDE, TOK), BF16), vm), (S((WIDE, TOK), BF16), vm), (S((34, 2, 2, 32, TOK), BF16), vm),
        (S((3, TOK, WIDE), BF16), vm), (S((TOK, WIDE), F32), vm), (S((TOK, WIDE), BF16), vm),
        (S((2, TOK, 2176), BF16), vm), (S((TOK, WIDE), BF16), vm),
    ]
    return pl.pallas_call(
        forward_kernel,
        out_shape=tuple(o[0] for o in outs),
        in_specs=[here] * 4 + [vm] * 4,
        out_specs=tuple(o[1] for o in outs),
        scratch_shapes=[
            V((2, 4, 4, 2, 16, 4608), BF16), V((2, 4, 4, 2, 16, 4352), BF16), V((2, 4, 4, 2, 2, 32, WIDE), BF16),
            V((2, 4, 4, 2, 2, 16, 512), BF16), V((4, 4, 512, 128), F32), V((256, WIDE), BF16), V((1, FF), F32),
            V((TOK, WIDE), BF16), V((TOK, WIDE), BF16), V((TOK, WIDE), BF16), V((TOK, FF), BF16), V((TOK, FF), F32),
            D((n, 3, 4)), D((n, 3, 4)), D((n, 4)), D((n, 4)), D((4,)), D((5,)),
        ],
        compiler_params=pltpu.CompilerParams(collective_id=0, has_side_effects=True, vmem_limit_bytes=62 * 2**20),
    )(p0, p1, p2, p3, tokens, cot, perm, bias)


def dealt():
    natural = lax.broadcasted_iota(jnp.int32, (WIDE, WIDE), 0)
    spot = lax.broadcasted_iota(jnp.int32, (WIDE, WIDE), 1)
    block, row = natural // 34, natural % 34
    target = jnp.where(row < 32, block * 32 + row, 1024 + (row - 32) * 32 + block)
    return ((target == spot) & (natural < REAL)).astype(BF16)


def hidden_left():
    a = lax.broadcasted_iota(jnp.int32, (256, 256), 0)
    b = lax.broadcasted_iota(jnp.int32, (256, 256), 1)
    j, r, s, q = a // 64, (a // 32) % 2, (a // 4) % 8, a % 4
    return (b == (q * 2 + r) * 32 + j * 8 + s).astype(BF16)


def causal_segments(seq_lengths, count):
    ends = jnp.cumsum(seq_lengths)
    position = jnp.arange(count, dtype=jnp.int32)
    segment = jnp.sum((position[:, None] >= ends[None, :]).astype(jnp.int32), axis=1)
    return (segment[:, None] == segment[None, :]) & (position[:, None] >= position[None, :])


def column_sum(rows):
    return jnp.sum(rows.astype(F32), axis=0)


def widen(t, n=WIDE):
    return jnp.pad(t, [(0, 0)] * (t.ndim - 1) + [(0, n - t.shape[-1])])


def own_pieces(q, core, moved_rows, left, vectors, qkv_weight):
    out_d, up_d, down_d = moved_rows[:34], moved_rows[34:170].reshape(34, 4, WIDE), moved_rows[170:306].reshape(4, 34, WIDE)
    up_left = dot(up_d[:, :, 1024:REAL].reshape(34, 256), left).astype(BF16)
    up_d = jnp.concatenate([up_d[:, :, :1024].reshape(34, 4096), up_left], axis=1)
    first = jnp.concatenate([widen(qkv_weight.reshape(34, 3, REAL)).reshape(34, 3456), out_d], axis=1)
    zl = q // 2
    p0 = lax.dynamic_slice(first, (zl * 16, core * 2304), (16, 2304))
    p1 = lax.dynamic_slice(up_d, (zl * 16, core * 2176), (16, 2176))
    p2 = lax.dynamic_slice(down_d, (q, 0, 0), (1, 32, WIDE))[0]
    bias = jnp.concatenate([widen(jnp.stack(vectors[:8]), 128).reshape(2, 512), widen(vectors[8].reshape(4, 34), 128).reshape(1, 512)], axis=0)
    rest = jnp.concatenate(
        [first[32:].reshape(18, 512), widen(up_d[32:], 4608).reshape(18, 512), widen(down_d[:, 32:], 1536).reshape(24, 512), bias, jnp.zeros((1, 512), BF16)],
        axis=0,
    )
    p3 = lax.dynamic_slice(rest, (q * 16, 0), (16, 512))
    return p0, p1, p2, p3


def specs():
    t, m, v = P(("fsdp", "rep"), None), P("fsdp", None), P("fsdp")
    return (t, t, t, v, v, m, v, v, m, v, v, v, m, v, m, v), (t, t, v, v, m, v, v, m, v, v, v, m, v, m, v)


def prepare(tokens, lengths, cotangent, attn_gain, attn_shift, qkv_weight, query_bias, value_bias, out_weight, out_bias, mlp_gain, mlp_shift, up_weight, up_bias, down_weight, down_bias):
    rank = lax.axis_index("rep")
    core = rank % 2
    perm = dealt()
    left = hidden_left()
    vectors = [attn_gain, attn_shift, query_bias, value_bias, out_bias, mlp_gain, mlp_shift, down_bias, up_bias]
    stacked = jnp.concatenate([out_weight, up_weight.reshape(136, REAL), down_weight, jnp.zeros((14, REAL), BF16), tokens, cotangent], axis=0)
    stacked = dot(stacked, perm[:REAL]).astype(BF16)
    pieces = own_pieces(rank, core, stacked, left, vectors, qkv_weight)
    bias = jnp.where(causal_segments(lengths[0], TOK), 0.0, excluded).astype(F32)
    return pieces, stacked[320:480], stacked[480:640], perm, left, bias


def scatter_units():
    out = [(2, g, 384 * g, 256, 128) for g in range(3)]
    out += [(1, 0, 0, 384, 384), (1, 1, 768, 384, 384), (1, 2, 1536, 384, 256)]
    out += [(0, g, 768 * g, 384, 384) for g in range(3)]
    return out + [(3, 0, 0, 256, 256)]


ROWS = (16, 16, 32, 16)
CHUNK_OF = {2: 0, 1: 1, 0: 2, 3: 3}


def block_dims(order, phase):
    free = order[phase + 1 :]
    dims = []
    if "z" in free:
        dims.append(2)
    if "x" in free:
        dims.append(4)
    if "y" in free:
        dims.append(4)
    if "z" in free:
        dims.append(2)
    return tuple(dims)


def part(ref, idx, cols):
    every = slice(None)
    z = idx["z"]
    zh, zl = (every, every) if z is None else (z // 2, lax.rem(z, 2))
    x = every if idx["x"] is None else idx["x"]
    y = every if idx["y"] is None else idx["y"]
    return ref.at[zh, x, y, zl, :, pl.ds(cols[0], cols[1])]


def backward_kernel(
    g0, g1, v1, v2, vecs, lt, nst, actt, qkv, resid, hg, tokens, cot, perm, bias,
    o0, o1, o2, o3, grad, *scratch,
):
    U = scatter_units()
    at, core = place()
    other = 1 - core
    me = device(at, core)
    sibling = device(at, other)
    partner_at = {**at, "z": at["z"] + 1 - 2 * lax.rem(at["z"], 2)}
    partner, diagonal = device(partner_at, core), device(partner_at, other)
    near = {(a, s): device(moved(at, a, s), core) for a in AXES for s in (1, -1)}
    s = list(scratch)
    sums = s[:4]
    sactt, scot, snst, shg, slt0, slt1, sr1, spr = s[4:12]
    wbuf, wo, dn, rgrad, r1, gh, left, pr, small = s[12:21]
    del s[:21]
    bufs = {}
    for u in range(len(U)):
        for p in range(3):
            bufs[u, p] = s[:2]
            del s[:2]
    send, recv, xsend, xrecv, rsend, rrecv, lsem, wsem = s
    meet(list(near.values()) + [sibling, diagonal])
    pending = []
    exchange = {}

    def give(i, src, dst):
        c = pltpu.make_async_remote_copy(src_ref=src, dst_ref=dst, send_sem=xsend.at[i], recv_sem=xrecv.at[i], device_id=sibling, device_id_type=MESH)
        c.start()
        pending.append(c)
        exchange[i] = c

    give(0, actt.at[pl.ds(0, 32), :, other], sactt)
    give(1, cot, scot)
    give(2, nst, snst)
    give(3, hg.at[other], shg)
    give(4, lt.at[0], slt0)
    give(5, lt.at[other], slt1)

    def block(u, phase, pos):
        order = ORDERS[U[u][1]][::-1]
        idx = {a: at[a] for a in AXES}
        idx[order[phase]] = pos
        for a in order[phase + 1 :]:
            idx[a] = None
        return idx

    def info(u, phase):
        w, g, c0, h0, h1 = U[u]
        axis = ORDERS[g][::-1][phase]
        pos = at[axis]
        pp, pm, po = (lax.rem(pos + i, 4) for i in (1, 3, 2))
        return w, (c0, h0), (c0 + h0, h1), near[axis, 1], near[axis, -1], pos, pp, pm, po

    def copies(u, phase):
        w, A, B, plus, minus, pos, pp, pm, po = info(u, phase)
        P_ = sums[w]
        ba, bb = bufs[u, phase]
        blk = lambda p, cols: part(P_, block(u, phase, p), cols)
        plan = [
            (blk(po, A), ba.at[0], plus), (blk(po, B), bb.at[0], minus), (blk(pp, B), bb.at[1], plus),
            (blk(pm, A), ba.at[1], minus), (blk(pp, A), ba.at[2], plus), (blk(pm, B), bb.at[2], minus),
        ]
        return [
            pltpu.make_async_remote_copy(src_ref=a, dst_ref=b, send_sem=send.at[u, phase, i], recv_sem=recv.at[u, phase, i], device_id=d, device_id_type=MESH)
            for i, (a, b, d) in enumerate(plan)
        ]

    live = {}

    def step_a(u, phase):
        cs = live[u, phase] = copies(u, phase)
        for c in cs[:4]:
            c.start()
        pending.extend(cs)

    def add(ref, *terms):
        t = ref[...].astype(F32)
        for o in terms:
            t = t + o[...].astype(F32)
        ref[...] = t.astype(BF16)

    def step_b(u, phase):
        w, A, B, plus, minus, pos, pp, pm, po = info(u, phase)
        cs = live[u, phase]
        ba, bb = bufs[u, phase]
        cs[0].wait_recv()
        add(part(sums[w], block(u, phase, pp), A), ba.at[0])
        cs[4].start()
        cs[1].wait_recv()
        add(part(sums[w], block(u, phase, pm), B), bb.at[0])
        cs[5].start()

    def step_c(u, phase):
        w, A, B, plus, minus, pos, pp, pm, po = info(u, phase)
        cs = live[u, phase]
        ba, bb = bufs[u, phase]
        cs[3].wait_recv()
        cs[4].wait_recv()
        add(part(sums[w], block(u, phase, pos), A), ba.at[1], ba.at[2])
        cs[2].wait_recv()
        cs[5].wait_recv()
        add(part(sums[w], block(u, phase, pos), B), bb.at[1], bb.at[2])

    outs = (o0, o1, o2, o3)

    def out_part(w, zl, c, cols):
        if w < 2:
            return outs[w].at[zl, :, pl.ds(pl.multiple_of(c * HALF[w] + cols[0], 128), cols[1])]
        return outs[w].at[zl, c, :, pl.ds(cols[0], cols[1])]

    local = []

    def share(u):
        w, g, c0, h0, h1 = U[u]
        src = part(sums[w], at, (c0, h0 + h1))
        dst = out_part(w, lax.rem(at["z"], 2), core, (c0, h0 + h1))
        c = pltpu.make_async_copy(src, dst, lsem.at[u])
        c.start()
        local.append(c)
        for i, dev in enumerate((sibling, partner, diagonal)):
            c = pltpu.make_async_remote_copy(src_ref=src, dst_ref=dst, send_sem=rsend.at[u, i], recv_sem=rrecv.at[u, i], device_id=dev, device_id_type=MESH)
            c.start()
            pending.append(c)

    def share_wait(u):
        w, g, c0, h0, h1 = U[u]
        zl = lax.rem(at["z"], 2)
        src = part(sums[w], at, (c0, h0 + h1))
        for i, (z, c) in enumerate(((zl, other), (1 - zl, core), (1 - zl, other))):
            pltpu.make_async_remote_copy(
                src_ref=src, dst_ref=out_part(w, z, c, (c0, h0 + h1)), send_sem=rsend.at[u, i], recv_sem=rrecv.at[u, i], device_id=me, device_id_type=MESH
            ).wait_recv()

    chunks = [[u for u in range(len(U)) if CHUNK_OF[U[u][0]] == c] for c in range(4)]

    def comm(c, k):
        for u in chunks[c]:
            if k == 0:
                step_a(u, 0)
            elif k in (1, 3, 5):
                step_b(u, k // 2)
            elif k in (2, 4):
                step_c(u, k // 2 - 1)
                step_a(u, k // 2)
            elif k == 6:
                step_c(u, 2)
                share(u)
            else:
                share_wait(u)

    def over_blocks(body):
        def step(i, carry):
            body(i // 4, lax.rem(i, 4), i)
            return carry
        lax.fori_loop(0, 8, step, 0)

    def down_weight():
        exchange[0].wait_recv()
        exchange[1].wait_recv()
        def body(zh, x, i):
            mine = actt[pl.ds(4 * i, 4), :, core].reshape(256, TOK)
            theirs = sactt[pl.ds(4 * i, 4)].reshape(256, TOK)
            for c in (0, 384, 768):
                t = dot(mine, cot[:, c : c + 384]) + dot(theirs, scot[:, c : c + 384])
                sums[2][zh, x, :, :, :, c : c + 384] = t.astype(BF16).reshape(4, 2, 32, 384)
        over_blocks(body)

    def up_weight():
        exchange[2].wait_recv()
        exchange[3].wait_recv()
        def body(zh, x, i):
            rows = pl.ds(pl.multiple_of(128 * i, 128), 128)
            mine, theirs = nst[rows, :], snst[rows, :]
            for c, n in ((0, 768), (768, 768), (1536, 640)):
                t = dot(mine, hg[core, :, c : c + n]) + dot(theirs, shg[:, c : c + n])
                sums[1][zh, x, :, :, :, c : c + n] = t.astype(BF16).reshape(4, 2, 16, n)
        over_blocks(body)

    def first_weight():
        for i in (4, 5, 6):
            exchange[i].wait_recv()
        def body(zh, x, i):
            rows = pl.ds(pl.multiple_of(128 * i, 128), 128)
            for c in (0, 768, 1536):
                for lo, n in ((c, 768),) if c != 768 else ((768, 384), (1152, 384)):
                    mine, theirs = (lt[0, rows, :], slt0[rows, :]) if lo < WIDE else (lt[core, rows, :], slt1[rows, :])
                    t = dot(mine, r1[core, :, lo : lo + n]) + dot(theirs, sr1[:, lo : lo + n])
                    sums[0][zh, x, :, :, :, lo : lo + n] = t.astype(BF16).reshape(4, 2, 16, n)
        over_blocks(body)

    fetched = {}

    def fetch(ref, i, n):
        if i < 8:
            b = i % 2
            fetched[i] = pltpu.make_async_copy(ref.at[i // 4, i % 4, :, :, :, pl.ds(0, n)], wbuf.at[b, :, :, :, pl.ds(0, n)], wsem.at[b])
            fetched[i].start()

    def second_norm_part(i):
        def run():
            if i == 0:
                fetch(g1, 0, FF)
                fetch(g1, 1, FF)
            if i < 8:
                fetched[i].wait()
                b = i % 2
                t = dot_nt(hg[0], wbuf[b, :, :, :, :2176].reshape(128, 2176)) + dot_nt(hg[1], wbuf[b, :, :, :, 2176:].reshape(128, 2176))
                fetch(g1, i + 2, FF)
            else:
                t = dot_nt(hg[0], v2[:, :2176]) + dot_nt(hg[1], v2[:, 2176:])
            dn[:, 128 * i : 128 * i + 128] = t
        return run

    def norm_back(values, gain):
        xhat, r = centred(values)
        e = dn[...]
        eg = e * gain
        m1 = jnp.sum(eg, axis=-1, keepdims=True) * (1.0 / REAL)
        m2 = jnp.sum(eg * xhat, axis=-1, keepdims=True) * (1.0 / REAL)
        back = jnp.where(iota((1, WIDE), 1) < REAL, r * (eg - m1 - xhat * m2), 0.0)
        return back, jnp.sum(e * xhat, axis=0, keepdims=True), jnp.sum(e, axis=0, keepdims=True)

    def total(t):
        return jnp.sum(t.astype(F32), axis=0, keepdims=True)

    def second_norm():
        back, gain_sum, shift_sum = norm_back(resid[...], vecs[5:6, :])
        t = cot[...].astype(F32) + back
        rgrad[...] = t
        low = t.astype(BF16)
        r1[1, :, WIDE:] = low
        small[4:5, :] = total(low)
        small[5:6, :] = gain_sum
        small[6:7, :] = shift_sum
        small[7:8, :] = total(cot[...])

    wo_copy = pltpu.make_async_copy(g0.at[:, :, :, :, :, pl.ds(3 * WIDE, WIDE)], wo, wsem.at[2])
    wo_copy.start()

    def attended_back():
        wo_copy.wait()
        low = r1[1, :, WIDE:]
        a = jnp.concatenate([dot_nt(low, wo[...].reshape(1024, WIDE)), dot_nt(low, v1[:, 3 * WIDE :])], axis=1).astype(BF16)
        gh[...] = dot_nt(a, perm[...]).astype(BF16)

    def attention_back(pair):
        def run():
            lanes = pl.ds(128 * pair, 128)
            q, k, v, g = qkv[0, :, lanes], qkv[1, :, lanes], qkv[2, :, lanes], gh[:, lanes]
            low_half = iota((1, 128), 1) < 64
            dq = jnp.zeros((TOK, 128), F32)
            dk, dv = dq, dq
            for half in range(2):
                mask = low_half if half == 0 else jnp.logical_not(low_half)
                pick = lambda t: jnp.where(mask, t, jnp.zeros_like(t))
                qh, kh, vh, gg = pick(q), pick(k), pick(v), pick(g)
                sc = dot_nt(q, kh) * 0.125 + bias[0]
                e = jnp.exp(sc - jnp.max(sc, axis=1, keepdims=True))
                p = e / jnp.sum(e, axis=1, keepdims=True)
                dp = dot_nt(g, vh)
                ds = (p * (dp - jnp.sum(p * dp, axis=1, keepdims=True))).astype(BF16)
                dq = dq + dot(ds, kh)
                sc = dot_nt(k, qh) * 0.125 + bias[1]
                e = jnp.exp(sc - jnp.max(sc, axis=0, keepdims=True))
                p = e / jnp.sum(e, axis=0, keepdims=True)
                dp = dot_nt(v, gg)
                ds = (p * (dp - jnp.sum(p * dp, axis=0, keepdims=True))).astype(BF16)
                dk = dk + dot(ds, qh)
                dv = dv + dot(p.astype(BF16), gg)
            lo = 128 * pair
            dq, dk, dv = (dq * 0.125).astype(BF16), (dk * 0.125).astype(BF16), dv.astype(BF16)
            r1[0, :, lo : lo + 128] = dq
            r1[0, :, WIDE + lo : WIDE + lo + 128] = dk
            r1[1, :, lo : lo + 128] = dv
            small[2:3, lo : lo + 128] = total(dq)
            small[3:4, lo : lo + 128] = total(dv)
        return run

    def give_first():
        give(6, r1.at[other], sr1)

    def first_norm_part(i):
        def run():
            if i == 0:
                fetch(g0, 0, 3 * WIDE)
                fetch(g0, 1, 3 * WIDE)
            if i < 8:
                fetched[i].wait()
                b = i % 2
                t = dot_nt(r1[0], wbuf[b, :, :, :, :2304].reshape(128, 2304)) + dot_nt(r1[1, :, :WIDE], wbuf[b, :, :, :, 2304:3456].reshape(128, WIDE))
                fetch(g0, i + 2, 3 * WIDE)
            else:
                t = dot_nt(r1[0], v1[:, :2304]) + dot_nt(r1[1, :, :WIDE], v1[:, 2304:3456])
            dn[:, 128 * i : 128 * i + 128] = t
        return run

    def first_norm():
        back, gain_sum, shift_sum = norm_back(tokens[...].astype(F32), vecs[0:1, :])
        rgrad[...] = rgrad[...] + back
        small[0:1, :] = gain_sum
        small[1:2, :] = shift_sum

    def natural_grad():
        t = rgrad[...]
        high = t.astype(BF16)
        t = t - high.astype(F32)
        mid = t.astype(BF16)
        low = (t - mid.astype(F32)).astype(BF16)
        grad[...] = dot_nt(high, perm[...]) + dot_nt(mid, perm[...]) + dot_nt(low, perm[...])

    def left_rows(t):
        def run():
            def put(i, values):
                left[i // 16, pl.ds(i % 16, 32, stride=16), :] = values

            tail = pl.ds(1024, 64)
            for j in range(9):
                lane = 512 * j + 128 * t
                rhs = r1[0, :, lane : lane + 128] if lane < 2304 else r1[1, :, lane - 2304 : lane - 2176]
                v = dot(lt[1 if lane >= 3 * WIDE else 0, tail, :], rhs)
                put(j, v[:32])
                put(9 + j, v[32:])
                if lane < FF:
                    rhs = hg[0, :, lane : lane + 128] if lane < 2176 else hg[1, :, lane - 2176 : lane - 2048]
                    v = dot(nst[tail, :], rhs)
                else:
                    v = jnp.zeros((64, 128), F32)
                put(18 + j, v[:32])
                put(27 + j, v[32:])
            for j in range(3):
                lane = 512 * j + 128 * t
                for b in range(2):
                    v = dot(actt[32 + b].reshape(128, TOK), cot[:, lane : lane + 128]) if lane < WIDE else jnp.zeros((128, 128), F32)
                    for i in range(4):
                        put(36 + 3 * (4 * b + i) + j, v[32 * i : 32 * i + 32])
            pick, own = dealt_pick()
            for i in range(2):
                v = small[4 * i + t : 4 * i + t + 1, :].astype(BF16)
                if i == 0 and t >= 2:
                    v = dot(v, perm[...]).astype(BF16)
                put(60 + i, dot_nt((own * v.astype(F32)).astype(BF16), pick))
            pick, own = hidden_pick(t)
            v = jnp.concatenate([total(hg[0]), total(hg[1])], axis=1)
            put(62, dot_nt((own * v).astype(BF16), pick))
            put(63, jnp.zeros((32, 128), F32))
            for zl in range(2):
                sums[3][:, :, :, zl, :, 128 * t : 128 * t + 128] = left[2 * zl + core].reshape(2, 4, 4, 16, 128).astype(BF16)
                pr[:, :, :, zl, :, 128 * t : 128 * t + 128] = left[2 * zl + other].reshape(2, 4, 4, 16, 128).astype(BF16)
        return run

    def give_left():
        give(7, pr, spr)

    def take_left():
        exchange[7].wait_recv()
        def body(zh, x, i):
            sums[3][zh, x] = (sums[3][zh, x].astype(F32) + spr[zh, x].astype(F32)).astype(BF16)
        over_blocks(body)

    C = lambda c, k: (lambda: comm(c, k))
    n2 = [second_norm_part(i) for i in range(9)]
    at_ = [attention_back(i) for i in range(9)]
    n1 = [first_norm_part(i) for i in range(9)]
    script = [down_weight, C(0, 0), up_weight, C(1, 0)] + n2 + [second_norm, C(0, 1), attended_back, C(1, 1)]
    script += at_[:3] + [C(0, 2)] + at_[3:6] + [C(1, 2)] + at_[6:] + [give_first, C(0, 3), C(1, 3)]
    script += [first_weight, C(2, 0)] + n1[:5] + [C(0, 4), C(1, 4)] + n1[5:] + [first_norm] + [left_rows(t) for t in range(4)] + [give_left]
    script += [C(2, 1), C(0, 5), C(1, 5), take_left, C(3, 0), natural_grad, C(2, 2), C(0, 6), C(1, 6), C(3, 1), C(2, 3), C(3, 2)]
    script += [C(2, 4), C(3, 3), C(2, 5), C(3, 4), C(2, 6), C(3, 5), C(3, 6), C(0, 7), C(1, 7), C(2, 7), C(3, 7)]
    for f in script:
        f()
    for c in local:
        c.wait()
    for c in pending:
        c.wait_send()


def backward_call(*ops):
    U = scatter_units()
    V, D, S = pltpu.VMEM, pltpu.SemaphoreType.DMA, jax.ShapeDtypeStruct
    here, vm = pl.BlockSpec(memory_space=pl.ANY), pl.BlockSpec(memory_space=pltpu.VMEM)
    scratch = [V((2, 4, 4, 2, 16, 2304), BF16), V((2, 4, 4, 2, 16, 2176), BF16), V((2, 4, 4, 2, 32, WIDE), BF16), V((2, 4, 4, 2, 16, 512), BF16)]
    scratch += [V((32, 2, 32, TOK), BF16), V((TOK, WIDE), BF16), V((WIDE, TOK), BF16), V((TOK, 2176), BF16), V((WIDE, TOK), BF16), V((WIDE, TOK), BF16)]
    scratch += [V((TOK, 2304), BF16), V((2, 4, 4, 2, 16, 512), BF16)]
    scratch += [V((2, 4, 2, 16, FF), BF16), V((2, 4, 4, 2, 16, WIDE), BF16), V((TOK, WIDE), F32), V((TOK, WIDE), F32), V((2, TOK, 2304), BF16)]
    scratch += [V((TOK, WIDE), BF16), V((4, 512, 128), F32), V((2, 4, 4, 2, 16, 512), BF16), V((8, WIDE), F32)]
    for w, g, c0, h0, h1 in U:
        for p in range(3):
            dims = block_dims(ORDERS[g][::-1], p)
            scratch += [V((3,) + dims + (ROWS[w], h0), BF16), V((3,) + dims + (ROWS[w], h1), BF16)]
    n = len(U)
    scratch += [D((n, 3, 6)), D((n, 3, 6)), D((8,)), D((8,)), D((n, 3)), D((n, 3)), D((n,)), D((3,))]
    return pl.pallas_call(
        backward_kernel,
        out_shape=(S((2, 16, 4608), BF16), S((2, 16, FF), BF16), S((2, 2, 32, WIDE), BF16), S((2, 2, 16, 512), BF16), S((TOK, WIDE), F32)),
        in_specs=[here] * 2 + [vm] * 13,
        out_specs=(here,) * 4 + (vm,),
        scratch_shapes=scratch,
        compiler_params=pltpu.CompilerParams(collective_id=1, has_side_effects=True, vmem_limit_bytes=63 * 2**20),
    )(*ops)


def body(*args):
    pieces, tokens, cot, perm, turn, bias = prepare(*args)
    g0, g1, g2, g3, v1, v2, vecs, lt, nst, actt, qkv, resid, ns, hg, layer_out = forward_call(*pieces, tokens, cot, perm, bias)
    both = jnp.stack([bias, bias.T])
    s0, s1, s2, s3, grad = backward_call(g0, g1, v1, v2, vecs, lt, nst, actt, qkv, resid, hg, tokens, cot, perm, both)
    left = s3.reshape(64, 512)
    first = jnp.concatenate([s0.reshape(32, 4608), left[:18].reshape(2, 4608)], axis=0)
    up_d = jnp.concatenate([s1.reshape(32, FF), left[18:36].reshape(2, 4608)[:, :FF]], axis=0)
    up_left = dot_nt(up_d[:, 4096:], turn).astype(BF16).reshape(34, 4, 64)
    up_d = widen(jnp.concatenate([up_d[:, :4096].reshape(34, 4, 1024), up_left], axis=2))
    down_d = jnp.concatenate([s2.reshape(4, 32, WIDE), left[36:60].reshape(4, 2, 1536)[:, :, :WIDE]], axis=1)
    stacked = jnp.concatenate([first[:, 3 * WIDE :], up_d.reshape(136, WIDE), down_d.reshape(136, WIDE)], axis=0)
    stacked = dot_nt(stacked, perm[:REAL])
    small = left[60:62].reshape(8, 128)[:, :34].astype(F32)
    units = left[62].reshape(4, 128)[:, :34].reshape(136).astype(F32)
    qkv_grad = first[:, : 3 * WIDE].reshape(34, 3, WIDE)[:, :, :REAL].reshape(34, 3 * REAL).astype(F32)
    return (
        layer_out[:, :REAL], grad[:, :REAL], small[0], small[1], qkv_grad, small[2], small[3], stacked[:34], small[4],
        small[5], small[6], stacked[34:170].reshape(34, FF), units, stacked[170:], small[7],
    )


def solution(mesh):
    ins, outs = specs()
    return jax.shard_map(body, mesh=mesh, in_specs=ins, out_specs=outs, check_vma=False)
```

```python
import jax
import jax.numpy as jnp
import ml_dtypes
import numpy as np
from jax import lax
from jax.experimental import pallas as pl
from jax.experimental.pallas import tpu as pltpu
from jax.sharding import PartitionSpec as P

MESH = pl.DeviceIdType.MESH
F32, BF16 = jnp.float32, jnp.bfloat16
AXES = "xyz"
ORDERS = ("xyz", "yzx", "zxy")
TOK = 160
WIDE = 1152
REAL = 1088
FF = 4352
epsilon = 1e-05
excluded = -1000000000.0
PER_STEP = 3
ROOT = 0.7978845608028654


def place():
    f = lax.axis_index("fsdp")
    r = lax.axis_index("rep")
    return dict(x=(f // 4) % 4, y=f % 4, z=(f // 16) * 2 + r // 2), r % 2


def device(at, core):
    z = at["z"]
    return ((z // 2) * 16 + at["x"] * 4 + at["y"], (z % 2) * 2 + core)


def moved(at, axis, step):
    return {**at, axis: lax.rem(at[axis] + step + 4, 4)}


def meet(devices):
    barrier = pltpu.get_barrier_semaphore()
    for d in devices:
        pl.semaphore_signal(barrier, inc=1, device_id=d, device_id_type=MESH)
    pl.semaphore_wait(barrier, len(devices))


def dot(a, b):
    return jnp.dot(a, b, preferred_element_type=F32)


def dot_nt(a, b):
    return lax.dot_general(a, b, (((1,), (1,)), ((), ())), preferred_element_type=F32)


def iota(shape, dim):
    return lax.broadcasted_iota(jnp.int32, shape, dim)


def eye(n):
    return jnp.where(iota((n, n), 0) == iota((n, n), 1), 1.0, 0.0).astype(BF16)


def dealt_pick():
    r, c = iota((128, WIDE), 0), iota((128, WIDE), 1)
    want = jnp.where(c < 1024, c & 31, jnp.where(c < REAL, 32 + ((c - 1024) >> 5), -1))
    s, c = iota((32, WIDE), 0), iota((32, WIDE), 1)
    owner = jnp.where(c < 1024, c >> 5, c & 31)
    return jnp.where(r == want, 1.0, 0.0).astype(BF16), jnp.where(s == owner, 1.0, 0.0)


def hidden_pick(k):
    r, c = iota((128, FF), 0), iota((128, FF), 1)
    want = jnp.where(c < 4096, c & 31, 32 + (((c - 4096) >> 5) & 1))
    s, c = iota((32, FF), 0), iota((32, FF), 1)
    d = c - 4096
    owner = jnp.where(c < 4096, c >> 5, 4 * (d & 31) + (d >> 6))
    return jnp.where(r == want, 1.0, 0.0).astype(BF16), jnp.where(4 * s + k == owner, 1.0, 0.0)


def centred(values):
    valid = iota((1, WIDE), 1) < REAL
    average = jnp.sum(values, axis=-1, keepdims=True) * (1.0 / REAL)
    c = jnp.where(valid, values - average, 0.0)
    r = lax.rsqrt(jnp.sum(c * c, axis=-1, keepdims=True) * (1.0 / REAL) + epsilon)
    return c * r, r


def gather_chunks():
    whole = [
        [(3, 0, 0, 16, 0, 256, 256)],
        [(0, 0, 0, 16, 0, 256, 256), (0, 1, 0, 16, 512, 512, 384), (0, 2, 0, 16, 1408, 512, 384)],
        [(1, 0, 0, 16, 0, 384, 256), (1, 1, 0, 16, 640, 384, 384), (1, 2, 0, 16, 1408, 384, 384)],
        [(2, g, 0, 32, 384 * g, 256, 128) for g in range(3)],
    ]
    parts = [
        [(3, 0, 0, 16, 0, 256, 256)],
        [(0, 0, 0, 16, 0, 128, 128), (0, 1, 0, 16, 512, 256, 256), (0, 2, 0, 16, 1408, 256, 256)],
        [(0, 0, 0, 16, 256, 128, 128), (0, 1, 0, 16, 1024, 256, 128), (0, 2, 0, 16, 1920, 256, 128)],
        [(1, 0, 0, 16, 0, 256, 128), (1, 1, 0, 16, 640, 256, 128), (1, 2, 0, 16, 1408, 256, 128)],
        [(1, 0, 0, 16, 384, 128, 128), (1, 1, 0, 16, 1024, 256, 128), (1, 2, 0, 16, 1792, 256, 128)],
        [(2, g, 0, 16, 384 * g, 256, 128) for g in range(3)],
        [(2, g, 16, 16, 384 * g, 256, 128) for g in range(3)],
    ]
    return whole, parts


HALF = (2304, 2176)
PAIR = "pair"


def slot(ref, w, idx, core, rows, cols):
    z = idx["z"]
    every = slice(None)
    if z is None or z is PAIR:
        zh, zl = (every if z is None else 0), every
    else:
        zh, zl = z // 2, lax.rem(z, 2)
    x, y = (every if idx[a] is None else pl.ds(0, 2) if idx[a] is PAIR else idx[a] for a in "xy")
    if w < 2:
        return ref.at[zh, x, y, zl, :, pl.ds(pl.multiple_of(core * HALF[w] + cols[0], 128), cols[1])]
    return ref.at[zh, x, y, zl, core, pl.ds(rows[0], rows[1]), pl.ds(cols[0], cols[1])]


def forward_kernel(
    p0, p1, p2, p3, tokens_in, cot_in, perm_in, bias_in,
    g0, g1, g2, g3, out_v1, out_v2, out_vecs, out_lt, out_nst, out_actt, out_qkv, out_resid, out_hg, out,
    w1, w2, w3, rest, unpacked, v3, upb, nf, att, attd, act, gp, v1, v2, vecs, lt, nst, actt, qkv, resid, ns, hg,
    tokens, cot, perm, bias, send, recv, ssend, srecv, lsem, wsem, osem, isem,
):
    at, core = place()
    me = device(at, core)
    sibling = device(at, 1 - core)
    near = {(a, s): device(moved(at, a, s), core) for a in AXES for s in (1, -1)}
    across_ring = {a: device(moved(at, a, 2), core) for a in AXES}
    meet(list(near.values()) + list(across_ring.values()) + [sibling])
    ins, outs = (p0, p1, p2, p3), (g0, g1, g2, g3)
    whole, parts = gather_chunks()
    U = [u for c in whole + parts for u in c]
    ids, n = [], 0
    for c in whole + parts:
        ids.append(list(range(n, n + len(c))))
        n += len(c)
    whole_ids, part_ids = ids[: len(whole)], ids[len(whole) :]
    whole_ids_flat = [u for c in whole_ids for u in c]
    started = []

    def block(u, phase, pos):
        order = ORDERS[U[u][1]]
        idx = dict(at)
        for a in order[:phase]:
            idx[a] = None
        idx[order[phase]] = pos
        return idx

    many = len(whole_ids_flat)

    def number(u, phase, b):
        return 4 * u + 2 * phase + b if u < many else 4 * many + 2 * (u - many) + b

    def ref_of(u, idx, cols, c=None):
        w, g, r0, nr = U[u][:4]
        return slot(outs[w], w, idx, core if c is None else c, (r0, nr), cols)

    def remote(src, dst, dev, s, r):
        return pltpu.make_async_remote_copy(src_ref=src, dst_ref=dst, send_sem=s, recv_sem=r, device_id=dev, device_id_type=MESH)

    def ring(u, phase, b, ref, dev, src=None):
        i = number(u, phase, b)
        remote(ref if src is None else src, ref, dev, send.at[i], recv.at[i]).start()

    def spots(u, phase):
        w, g, r0, nr, c0, h0, h1 = U[u]
        axis = ORDERS[g][phase]
        pos = at[axis]
        return axis, pos, [lax.rem(pos + i, 4) for i in (1, 3, 2)], (c0, h0 + h1), (c0, h0), (c0 + h0, h1)

    def go(u, k):
        w, g, r0, nr, c0, h0, h1 = U[u]
        phase, b = divmod(k, 2)
        axis, pos, (pp, pm, po), full, A, B = spots(u, phase)
        plus, minus = near[axis, 1], near[axis, -1]
        if b == 0:
            src = ins[w].at[pl.ds(r0, nr), pl.ds(c0, h0 + h1)] if phase == 0 else None
            own = ref_of(u, block(u, phase, pos), full)
            ring(u, phase, 0, own, plus, src)
            ring(u, phase, 0, own, minus, src)
            if phase == 0:
                ring(u, 0, 1, own, across_ring[axis], src)
                started.append((u, 0, 1))
        else:
            ring(u, phase, 1, ref_of(u, block(u, phase, pm), A), plus)
            ring(u, phase, 1, ref_of(u, block(u, phase, pp), B), minus)
        started.append((u, phase, b))

    def in_flight(u, phase, b):
        axis, pos, others, full, A, B = spots(u, phase)
        ref = ref_of(u, block(u, phase, pos if b else PAIR), full)
        i = number(u, phase, b)
        return remote(ref, ref, me, send.at[i], recv.at[i])

    def arrive(u, k):
        in_flight(u, *divmod(k, 2)).wait_recv()

    def across(u, j):
        axis, pos, others, full, A, B = spots(u, 2)
        ref = ref_of(u, block(u, 2, ([pos] + others)[j]), full)
        remote(ref, ref, sibling, ssend.at[u - many], srecv.at[u - many]).start()

    def all_across(u, c):
        axis, pos, others, full, A, B = spots(u, 2)
        ref = ref_of(u, dict(x=None, y=None, z=None), full, c)
        return remote(ref, ref, me, ssend.at[u - many], srecv.at[u - many])

    def arrive_across(u):
        all_across(u, 1 - core).wait_recv()

    entries = []
    for i, (a, b) in enumerate(((perm_in, perm), (tokens_in, tokens), (bias_in, bias), (cot_in, cot))):
        c = pltpu.make_async_copy(a, b, isem.at[i])
        c.start()
        entries.append(c)
    own_copies = []
    for w in range(4):
        cols = (0, (2304, 2176, WIDE, 512)[w])
        rows = (0, (16, 16, 32, 16)[w])
        c = pltpu.make_async_copy(ins[w], slot(outs[w], w, at, core, rows, cols), lsem.at[w])
        c.start()
        own_copies.append(c)

    def early(c, k):
        def run():
            for u in whole_ids[c]:
                if k == 2:
                    arrive(u, 0)
                if k > 0:
                    arrive(u, k - 1)
                if k < 4:
                    go(u, k)
        return run

    def third(c):
        def run():
            for u in part_ids[c]:
                go(u, 4)
            for u in part_ids[c]:
                across(u, 0)
        return run

    def onward(c):
        def run():
            for u in part_ids[c]:
                arrive(u, 4)
                go(u, 5)
            for u in part_ids[c]:
                across(u, 1)
                across(u, 2)
        return run

    def last(c):
        def run():
            for u in part_ids[c]:
                arrive(u, 5)
                across(u, 3)
        return run

    loads = {}
    written = []

    def write(src, dst):
        def run():
            c = pltpu.make_async_copy(src, dst, osem.at[len(written)])
            c.start()
            written.append(c)
        return run


    def load(name, src, dst, i):
        loads[name] = pltpu.make_async_copy(src, dst, wsem.at[i])
        loads[name].start()

    def landed(c):
        for u in part_ids[c]:
            arrive_across(u)

    def weight(ref, lo, n):
        return ref[:, :, :, :, :, lo : lo + n].reshape(1024, n)

    def row(i):
        return vecs[i : i + 1, :]

    def stage_rest():
        for c in entries:
            c.wait()
        landed(0)
        load("rest", g3, rest, 3)
        loads["rest"].wait()
        for q in range(4):
            for t in range(4):
                piece = rest[:, :, :, q // 2, q % 2, :, 128 * t : 128 * t + 128].astype(F32)
                unpacked[t, q] = piece.reshape(512, 128)

    def gathered_row(i, t):
        return unpacked[t, i // 16, pl.ds(i % 16, 32, stride=16), :]

    def stage_vectors():
        pick, own = dealt_pick()
        rows = []
        for i in range(8):
            b = gathered_row(60 + i // 4, i % 4).astype(BF16)
            rows.append(jnp.sum(own * dot(b, pick), axis=0, keepdims=True))
        all_rows = jnp.concatenate(rows, axis=0)
        natural = dot_nt(all_rows.astype(BF16), perm[...])
        vecs[...] = jnp.concatenate([all_rows[:2], natural[2:4], all_rows[4:]], axis=0)

    def stage_units(k):
        def run():
            pick, own = hidden_pick(k)
            b = gathered_row(62, k).astype(BF16)
            t = jnp.sum(own * dot(b, pick), axis=0, keepdims=True)
            upb[...] = t if k == 0 else upb[...] + t
        return run

    def stage_left(w):
        def run():
            if w < 2:
                dst = (v1, v2)[w]
                for r in range(2):
                    for j in range(9):
                        for t in range(4):
                            lane = 512 * j + 128 * t
                            if lane < dst.shape[1]:
                                dst[32 * r : 32 * r + 32, lane : lane + 128] = gathered_row(18 * w + 9 * r + j, t).astype(BF16)
                dst[64:, :] = jnp.zeros((64, dst.shape[1]), BF16)
            else:
                for b in range(8):
                    for j in range(3):
                        for t in range(4):
                            lane = 512 * j + 128 * t
                            if lane < WIDE:
                                v3[32 * b : 32 * b + 32, lane : lane + 128] = gathered_row(36 + 3 * b + j, t).astype(BF16)
        return run

    def flipped(ref):
        parts = []
        for c in range(0, WIDE, 256):
            n = min(256, WIDE - c)
            parts.append((c, n, dot_nt(eye(n), ref[:, c : c + n]).astype(BF16)))
        return parts

    def stage_norm():
        xhat, r = centred(tokens[...].astype(F32))
        nf[...] = (xhat * row(0) + row(1)).astype(BF16)
        for c, n, t in flipped(nf):
            lt[0, c : c + n, :] = t

    def stage_load1():
        landed(1)
        landed(2)
        load("w1", g0, w1, 0)

    def stage_qkv(i):
        def run():
            if i == 0:
                loads["w1"].wait()
            for c in (0, 384, 768):
                lo = WIDE * i + c
                t = dot(nf[:, :1024], weight(w1, lo, 384)) + dot(nf[:, 1024:], v1[:, lo : lo + 384])
                if i != 1:
                    t = t + vecs[2 + i // 2 : 3 + i // 2, c : c + 384]
                qkv[i, :, c : c + 384] = t.astype(BF16)
        return run

    def stage_attention(pair):
        def run():
            lanes = pl.ds(128 * pair, 128)
            q, k, v = qkv[0, :, lanes], qkv[1, :, lanes], qkv[2, :, lanes]
            low_half = iota((1, 128), 1) < 64
            total = jnp.zeros((TOK, 128), F32)
            for half in range(2):
                mask = low_half if half == 0 else jnp.logical_not(low_half)
                pick = lambda t: jnp.where(mask, t, jnp.zeros_like(t))
                s = dot_nt(q, pick(k)) * 0.125 + bias[...]
                e = jnp.exp(s - jnp.max(s, axis=-1, keepdims=True))
                p = e / jnp.sum(e, axis=-1, keepdims=True)
                total = total + dot(p.astype(BF16), pick(v))
            att[:, lanes] = total.astype(BF16)
        return run

    def stage_out():
        attd[...] = dot(att[...], perm[...]).astype(BF16)
        for c in (0, 384, 768):
            lo = 3 * WIDE + c
            t = dot(attd[:, :1024], weight(w1, lo, 384)) + dot(attd[:, 1024:], v1[:, lo : lo + 384])
            resid[:, c : c + 384] = tokens[:, c : c + 384].astype(F32) + t + vecs[4:5, c : c + 384]
        for c, n, t in flipped(attd):
            lt[1, c : c + n, :] = t

    def stage_norm2():
        xhat, r = centred(resid[...])
        ns[...] = (xhat * row(5) + row(6)).astype(BF16)
        for c, n, t in flipped(ns):
            nst[c : c + n, :] = t

    def stage_load2():
        landed(3)
        landed(4)
        load("w2", g1, w2, 1)

    def stage_up(half, c, n):
        def run():
            if half == 0 and c == 0:
                loads["w2"].wait()
            lo = 2176 * half + c
            u = dot(ns[:, :1024], weight(w2, lo, n)) + dot(ns[:, 1024:], v2[:, lo : lo + n]) + upb[:, lo : lo + n]
            t = jnp.tanh(ROOT * (u + 0.044715 * u * u * u))
            a = (0.5 * u * (1.0 + t)).astype(BF16)
            act[:, lo : lo + n] = a
            gp[:, lo : lo + n] = 0.5 * (1.0 + t) + 0.5 * u * (1.0 - t * t) * (ROOT * (1.0 + 3 * 0.044715 * u * u))
            for j in range(0, n, 128):
                f = lo + j
                flip = dot_nt(eye(128), a[:, j : j + 128]).astype(BF16)
                if f < 4096:
                    actt[f // 128] = flip.reshape(2, 2, 32, TOK)
                else:
                    actt[f // 128] = flip.reshape(2, 2, 32, TOK)
        return run

    def stage_load3(i):
        def run():
            landed(5 + i)
            r = pl.ds(16 * i, 16)
            load(f"w3{i}", g2.at[:, :, :, :, :, r, :], w3.at[:, :, :, :, :, r, :], 2 + 2 * i)
        return run

    def stage_down(c):
        def run():
            if c == 0:
                loads["w30"].wait()
                loads["w31"].wait()
            t = dot(act[:, :4096], w3[:, :, :, :, :, :, c : c + 384].reshape(4096, 384))
            t = t + dot(act[:, 4096:], v3[:, c : c + 384])
            attd[:, c : c + 384] = (resid[:, c : c + 384] + t + vecs[7:8, c : c + 384]).astype(BF16)
        return run

    def stage_result():
        out[...] = dot_nt(attd[...], perm[...]).astype(BF16)

    def stage_hidden(zh, x):
        def run():
            f = (zh * 4 + x) * 512
            d = dot_nt(cot[...], w3[zh, x].reshape(512, WIDE))
            g = (d * gp[:, f : f + 512]).astype(BF16)
            put_hidden(f, 512, g)
        return run

    def put_hidden(f, n, g):
        if f + n <= 2176:
            hg[0, :, f : f + n] = g
        elif f >= 2176:
            hg[1, :, f - 2176 : f - 2176 + n] = g
        else:
            m = 2176 - f
            hg[0, :, f:2176] = g[:, :m]
            hg[1, :, : n - m] = g[:, m:]

    def stage_hidden_left():
        d = dot_nt(cot[...], v3[...])
        put_hidden(4096, 256, (d * gp[:, 4096:]).astype(BF16))

    ups = [stage_up(h, c, n) for h in range(2) for c, n in ((0, 512), (512, 512), (1024, 512), (1536, 640))]
    lefts = [stage_left(w) for w in range(3)]
    work = {
        0: [stage_rest, stage_vectors] + [stage_units(k) for k in range(4)] + [stage_norm] + lefts + [write(v1, out_v1), write(v2, out_v2), write(vecs, out_vecs)],
        2: [stage_load1] + [stage_qkv(i) for i in range(3)] + [write(qkv, out_qkv)] + [stage_attention(i) for i in range(9)] + [stage_out, write(resid, out_resid), write(lt, out_lt), stage_norm2, write(nst, out_nst)],
        4: [stage_load2] + ups + [write(actt, out_actt)],
        5: [stage_load3(0)],
        6: [stage_load3(1)] + [stage_down(c) for c in (0, 384, 768)] + [stage_result] + [stage_hidden(zh, x) for zh in range(2) for x in range(4)] + [stage_hidden_left, write(hg, out_hg)],
    }
    queue = []

    def compute(n):
        for _ in range(min(n, len(queue))):
            queue.pop(0)()

    script = "e00 e10 e20 e30 own e02 e12 e22 e32 e03 e13 e23 e33 "
    script += "e04 t0 e14 t1 t2 e24 e34 t3 o0 o1 t4 o2 - t5 l0 - l1 - l2 - o3 - t6 - o4 - - l3 - l4 - o5 - - o6 - l5 - l6"
    waiting = []
    for word in script.split():
        if word == "own":
            for c in own_copies:
                c.wait()
        elif word == "-":
            compute(PER_STEP)
            for w in waiting:
                queue.extend(work.get(w, []))
            waiting = []
        elif word[0] == "e":
            early(int(word[1]), int(word[2]))()
        else:
            {"t": third, "o": onward, "l": last}[word[0]](int(word[1]))()
            if word[0] == "l":
                waiting.append(int(word[1]))
    for w in waiting:
        queue.extend(work.get(w, []))
    compute(len(queue))
    for c in written:
        c.wait()
    for u, phase, b in started:
        in_flight(u, phase, b).wait_send()
    for u in [u for c in part_ids for u in c]:
        all_across(u, core).wait_send()


def forward_call(p0, p1, p2, p3, tokens, cot, perm, bias):
    whole, parts = gather_chunks()
    n, m = sum(len(c) for c in whole), sum(len(c) for c in parts)
    D, V = pltpu.SemaphoreType.DMA, pltpu.VMEM
    here, vm = pl.BlockSpec(memory_space=pl.ANY), pl.BlockSpec(memory_space=pltpu.VMEM)
    S = jax.ShapeDtypeStruct
    kept = [
        ((128, 4608), BF16), ((128, FF), BF16), ((8, WIDE), F32), ((2, WIDE, TOK), BF16), ((WIDE, TOK), BF16),
        ((34, 2, 2, 32, TOK), BF16), ((3, TOK, WIDE), BF16), ((TOK, WIDE), F32), ((2, TOK, 2176), BF16),
    ]
    gathered = [(2, 4, 4, 2, 16, 4608), (2, 4, 4, 2, 16, FF), (2, 4, 4, 2, 2, 32, WIDE), (2, 4, 4, 2, 2, 16, 512)]
    scratch = [V(shape, BF16) for shape in gathered]
    scratch += [
        V((4, 4, 512, 128), F32), V((256, WIDE), BF16), V((1, FF), F32),
        V((TOK, WIDE), BF16), V((TOK, WIDE), BF16), V((TOK, WIDE), BF16), V((TOK, FF), BF16), V((TOK, FF), F32),
    ]
    scratch += [V(*k) for k in kept[:8]] + [V((TOK, WIDE), BF16), V(*kept[8])]
    scratch += [V((TOK, WIDE), BF16), V((TOK, WIDE), BF16), V((WIDE, WIDE), BF16), V((TOK, TOK), F32)]
    scratch += [D((4 * n + 2 * m,)), D((4 * n + 2 * m,)), D((m,)), D((m,)), D((4,)), D((5,)), D((len(kept),)), D((4,))]
    return pl.pallas_call(
        forward_kernel,
        out_shape=tuple(S(shape, BF16) for shape in gathered) + tuple(S(*k) for k in kept) + (S((TOK, WIDE), BF16),),
        in_specs=[here] * 8,
        out_specs=(here,) * 13 + (vm,),
        scratch_shapes=scratch,
        compiler_params=pltpu.CompilerParams(collective_id=0, has_side_effects=True, vmem_limit_bytes=62 * 2**20),
    )(p0, p1, p2, p3, tokens, cot, perm, bias)


def dealt():
    natural = np.arange(WIDE)
    block, row = natural // 34, natural % 34
    target = np.where(row < 32, block * 32 + row, 1024 + (row - 32) * 32 + block)
    target = jnp.asarray(np.where(natural < REAL, target, -1).astype(np.int32))
    return (target[:, None] == lax.broadcasted_iota(jnp.int32, (WIDE, WIDE), 1)).astype(BF16)


def hidden_left():
    a = np.arange(256)
    j, r, s, q = a // 64, (a // 32) % 2, (a // 4) % 8, a % 4
    target = jnp.asarray(((q * 2 + r) * 32 + j * 8 + s).astype(np.int32))
    return (target[:, None] == lax.broadcasted_iota(jnp.int32, (256, 256), 1)).astype(BF16)


def causal_segments(seq_lengths, count):
    ends = jnp.cumsum(seq_lengths)
    position = jnp.arange(count, dtype=jnp.int32)
    segment = jnp.sum((position[:, None] >= ends[None, :]).astype(jnp.int32), axis=1)
    return (segment[:, None] == segment[None, :]) & (position[:, None] >= position[None, :])


def column_sum(rows):
    return jnp.sum(rows.astype(F32), axis=0)


def widen(t, n=WIDE):
    return jnp.pad(t, [(0, 0)] * (t.ndim - 1) + [(0, n - t.shape[-1])])


def own_pieces(q, core, moved_rows, left, vectors, qkv_weight):
    out_d, up_d, down_d = moved_rows[:34], moved_rows[34:170].reshape(34, 4, WIDE), moved_rows[170:306].reshape(4, 34, WIDE)
    up_left = dot(up_d[:, :, 1024:REAL].reshape(34, 256), left).astype(BF16)
    up_d = jnp.concatenate([up_d[:, :, :1024].reshape(34, 4096), up_left], axis=1)
    first = jnp.concatenate([widen(qkv_weight.reshape(34, 3, REAL)).reshape(34, 3456), out_d], axis=1)
    zl = q // 2
    p0 = lax.dynamic_slice(first, (zl * 16, core * 2304), (16, 2304))
    p1 = lax.dynamic_slice(up_d, (zl * 16, core * 2176), (16, 2176))
    p2 = lax.dynamic_slice(down_d, (q, 0, 0), (1, 32, WIDE))[0]
    bias = jnp.concatenate([widen(jnp.stack(vectors[:8]), 128).reshape(2, 512), widen(vectors[8].reshape(4, 34), 128).reshape(1, 512)], axis=0)
    rest = jnp.concatenate(
        [first[32:].reshape(18, 512), widen(up_d[32:], 4608).reshape(18, 512), widen(down_d[:, 32:], 1536).reshape(24, 512), bias, jnp.zeros((1, 512), BF16)],
        axis=0,
    )
    p3 = lax.dynamic_slice(rest, (q * 16, 0), (16, 512))
    return p0, p1, p2, p3


def specs():
    t, m, v = P(("fsdp", "rep"), None), P("fsdp", None), P("fsdp")
    return (t, t, t, v, v, m, v, v, m, v, v, v, m, v, m, v), (t, t, v, v, m, v, v, m, v, v, v, m, v, m, v)


def prepare(tokens, lengths, cotangent, attn_gain, attn_shift, qkv_weight, query_bias, value_bias, out_weight, out_bias, mlp_gain, mlp_shift, up_weight, up_bias, down_weight, down_bias):
    rank = lax.axis_index("rep")
    core = rank % 2
    perm = dealt()
    left = hidden_left()
    vectors = [attn_gain, attn_shift, query_bias, value_bias, out_bias, mlp_gain, mlp_shift, down_bias, up_bias]
    stacked = jnp.concatenate([out_weight, up_weight.reshape(136, REAL), down_weight, jnp.zeros((14, REAL), BF16), tokens, cotangent], axis=0)
    stacked = dot(stacked, perm[:REAL]).astype(BF16)
    pieces = own_pieces(rank, core, stacked, left, vectors, qkv_weight)
    bias = jnp.where(causal_segments(lengths[0], TOK), 0.0, excluded).astype(F32)
    return pieces, stacked[320:480], stacked[480:640], perm, left, bias


def scatter_units():
    out = [(2, g, 384 * g, 256, 128) for g in range(3)]
    out += [(1, 0, 0, 384, 256), (1, 1, 640, 384, 384), (1, 2, 1408, 384, 384)]
    out += [(0, 0, 0, 256, 256), (0, 1, 512, 512, 384), (0, 2, 1408, 512, 384)]
    return out + [(3, 0, 0, 256, 256)]


ROWS = (16, 16, 32, 16)
CHUNK_OF = {2: 0, 1: 1, 0: 2, 3: 3}


def block_dims(order, phase):
    free = order[phase + 1 :]
    dims = []
    if "z" in free:
        dims.append(2)
    if "x" in free:
        dims.append(4)
    if "y" in free:
        dims.append(4)
    if "z" in free:
        dims.append(2)
    return tuple(dims)


def part(ref, idx, cols):
    every = slice(None)
    z = idx["z"]
    zh, zl = (every, every) if z is None else (z // 2, lax.rem(z, 2))
    x = every if idx["x"] is None else idx["x"]
    y = every if idx["y"] is None else idx["y"]
    return ref.at[zh, x, y, zl, :, pl.ds(cols[0], cols[1])]


def backward_kernel(
    g0, g1, *rest,
):
    given, (o0, o1, o2, o3, grad), scratch = rest[:13], rest[13:18], rest[18:]
    U = scatter_units()
    at, core = place()
    other = 1 - core
    me = device(at, core)
    sibling = device(at, other)
    partner_at = {**at, "z": at["z"] + 1 - 2 * lax.rem(at["z"], 2)}
    partner, diagonal = device(partner_at, core), device(partner_at, other)
    near = {(a, s): device(moved(at, a, s), core) for a in AXES for s in (1, -1)}
    s = list(scratch)
    held, isem = s[-14:-1], s[-1]
    del s[-14:]
    v1, v2, vecs, lt, nst, actt, qkv, resid, hg, tokens, cot, perm, bias = held
    lt_in, nst_in, actt_in, hg_in, cot_in = given[3], given[4], given[5], given[8], given[10]
    sums = s[:4]
    sactt, scot, snst, shg, slt0, slt1, sr1, spr = s[4:12]
    wbuf, wo, dn, rgrad, r1, gh, left, pr, small = s[12:21]
    del s[:21]
    bufs = {}
    for u in range(len(U)):
        for p in range(3):
            bufs[u, p] = s[:2]
            del s[:2]
    send, recv, xsend, xrecv, rsend, rrecv, lsem, wsem = s
    across_ring = {a: device(moved(at, a, 2), core) for a in AXES}
    meet(list(near.values()) + list(across_ring.values()) + [sibling, diagonal])
    pending = []
    exchange = {}

    def give(i, src, dst):
        c = pltpu.make_async_remote_copy(src_ref=src, dst_ref=dst, send_sem=xsend.at[i], recv_sem=xrecv.at[i], device_id=sibling, device_id_type=MESH)
        c.start()
        pending.append(c)
        exchange[i] = c

    loads = {}
    for i in (5, 10, 4, 8, 1, 7, 2, 0, 11, 6, 12, 3, 9):
        loads[i] = pltpu.make_async_copy(given[i], held[i], isem.at[i])
    for i in (5, 10):
        loads[i].start()
    give(0, actt_in.at[pl.ds(0, 32), :, other], sactt)
    give(1, cot_in, scot)
    give(2, nst_in, snst)
    give(3, hg_in.at[other], shg)
    for i in (4, 8, 1, 7, 2, 0, 11, 6, 12, 3, 9):
        loads[i].start()
    give(4, lt_in.at[0], slt0)
    give(5, lt_in.at[other], slt1)

    def need(*which):
        for i in which:
            loads[i].wait()

    def block(u, phase, pos):
        order = ORDERS[U[u][1]][::-1]
        idx = {a: at[a] for a in AXES}
        idx[order[phase]] = pos
        for a in order[phase + 1 :]:
            idx[a] = None
        return idx

    def info(u, phase):
        w, g, c0, h0, h1 = U[u]
        axis = ORDERS[g][::-1][phase]
        pos = at[axis]
        pp, pm, po = (lax.rem(pos + i, 4) for i in (1, 3, 2))
        return w, (c0, h0), (c0 + h0, h1), near[axis, 1], near[axis, -1], pos, pp, pm, po

    def copies(u, phase):
        w, A, B, plus, minus, pos, pp, pm, po = info(u, phase)
        P_ = sums[w]
        ba, bb = bufs[u, phase]
        blk = lambda p, cols: part(P_, block(u, phase, p), cols)
        far = across_ring[ORDERS[U[u][1]][::-1][phase]] if phase == 2 else None
        plan = [
            (blk(po, A), ba.at[0], far or plus), (blk(po, B), bb.at[0], far or minus), (blk(pp, B), bb.at[1], plus),
            (blk(pm, A), ba.at[1], minus), (blk(pp, A), ba.at[2], plus), (blk(pm, B), bb.at[2], minus),
        ]
        first = (1, 0, 0, 1, 1, 0)
        land = (0, 1, 3, 2, 2, 3)
        return [
            pltpu.make_async_remote_copy(src_ref=a, dst_ref=b, send_sem=send.at[u, phase, first[i]], recv_sem=recv.at[u, phase, land[i]], device_id=d, device_id_type=MESH)
            for i, (a, b, d) in enumerate(plan)
        ]

    def landed(u, phase, i):
        ref = bufs[u, phase][i].at[pl.ds(1, 2)]
        pltpu.make_async_remote_copy(src_ref=ref, dst_ref=ref, send_sem=send.at[u, phase, 0], recv_sem=recv.at[u, phase, 2 + i], device_id=me, device_id_type=MESH).wait_recv()

    def sent(u, phase):
        for i in range(2):
            ref = bufs[u, phase][i]
            pltpu.make_async_remote_copy(src_ref=ref, dst_ref=ref, send_sem=send.at[u, phase, 1 - i], recv_sem=recv.at[u, phase, i], device_id=me, device_id_type=MESH).wait_send()

    live = {}

    def step_a(u, phase):
        cs = live[u, phase] = copies(u, phase)
        for c in cs if phase == 2 else cs[:4]:
            c.start()

    def add(ref, *terms):
        t = ref[...].astype(F32)
        for o in terms:
            t = t + o[...].astype(F32)
        ref[...] = t.astype(BF16)

    def step_b(u, phase):
        w, A, B, plus, minus, pos, pp, pm, po = info(u, phase)
        cs = live[u, phase]
        ba, bb = bufs[u, phase]
        cs[0].wait_recv()
        add(part(sums[w], block(u, phase, pp), A), ba.at[0])
        cs[4].start()
        cs[1].wait_recv()
        add(part(sums[w], block(u, phase, pm), B), bb.at[0])
        cs[5].start()

    def step_c(u, phase):
        w, A, B, plus, minus, pos, pp, pm, po = info(u, phase)
        cs = live[u, phase]
        ba, bb = bufs[u, phase]
        far = 0 if phase == 2 else 1
        if phase == 2:
            cs[0].wait_recv()
            cs[1].wait_recv()
        landed(u, phase, 0)
        add(part(sums[w], block(u, phase, pos), A), *[ba.at[i] for i in range(far, 3)])
        landed(u, phase, 1)
        add(part(sums[w], block(u, phase, pos), B), *[bb.at[i] for i in range(far, 3)])

    outs = (o0, o1, o2, o3)

    def out_part(w, zl, c, cols):
        if w < 2:
            return outs[w].at[zl, :, pl.ds(pl.multiple_of(c * HALF[w] + cols[0], 128), cols[1])]
        return outs[w].at[zl, c, :, pl.ds(cols[0], cols[1])]

    local = []

    def share(u):
        w, g, c0, h0, h1 = U[u]
        src = part(sums[w], at, (c0, h0 + h1))
        dst = out_part(w, lax.rem(at["z"], 2), core, (c0, h0 + h1))
        c = pltpu.make_async_copy(src, dst, lsem.at[u])
        c.start()
        local.append(c)
        for i, dev in enumerate((sibling, partner, diagonal)):
            c = pltpu.make_async_remote_copy(src_ref=src, dst_ref=dst, send_sem=rsend.at[u, i], recv_sem=rrecv.at[u, i], device_id=dev, device_id_type=MESH)
            c.start()
            pending.append(c)

    def share_wait(u):
        w, g, c0, h0, h1 = U[u]
        zl = lax.rem(at["z"], 2)
        src = part(sums[w], at, (c0, h0 + h1))
        for i, (z, c) in enumerate(((zl, other), (1 - zl, core), (1 - zl, other))):
            pltpu.make_async_remote_copy(
                src_ref=src, dst_ref=out_part(w, z, c, (c0, h0 + h1)), send_sem=rsend.at[u, i], recv_sem=rrecv.at[u, i], device_id=me, device_id_type=MESH
            ).wait_recv()

    chunks = [[u for u in range(len(U)) if CHUNK_OF[U[u][0]] == c] for c in range(4)]

    def comm(c, k):
        for u in chunks[c]:
            if k == 0:
                step_a(u, 0)
            elif k in (1, 3):
                step_b(u, k // 2)
            elif k == 5:
                continue
            elif k in (2, 4):
                step_c(u, k // 2 - 1)
                step_a(u, k // 2)
            elif k == 6:
                step_c(u, 2)
                share(u)
            else:
                share_wait(u)

    def over_blocks(body):
        def step(i, carry):
            body(i // 4, lax.rem(i, 4), i)
            return carry
        lax.fori_loop(0, 8, step, 0)

    def down_weight():
        need(5, 10)
        exchange[0].wait_recv()
        exchange[1].wait_recv()
        def body(zh, x, i):
            mine = actt[pl.ds(4 * i, 4), :, core].reshape(256, TOK)
            theirs = sactt[pl.ds(4 * i, 4)].reshape(256, TOK)
            for c in (0, 384, 768):
                t = dot(mine, cot[:, c : c + 384]) + dot(theirs, scot[:, c : c + 384])
                sums[2][zh, x, :, :, :, c : c + 384] = t.astype(BF16).reshape(4, 2, 32, 384)
        over_blocks(body)

    def up_weight():
        need(4, 8)
        exchange[2].wait_recv()
        exchange[3].wait_recv()
        def body(zh, x, i):
            rows = pl.ds(pl.multiple_of(128 * i, 128), 128)
            mine, theirs = nst[rows, :], snst[rows, :]
            for c, n in ((0, 768), (768, 768), (1536, 640)):
                t = dot(mine, hg[core, :, c : c + n]) + dot(theirs, shg[:, c : c + n])
                sums[1][zh, x, :, :, :, c : c + n] = t.astype(BF16).reshape(4, 2, 16, n)
        over_blocks(body)

    def first_weight():
        for i in (4, 5, 6):
            exchange[i].wait_recv()
        def body(zh, x, i):
            rows = pl.ds(pl.multiple_of(128 * i, 128), 128)
            for c in (0, 768, 1536):
                for lo, n in ((c, 768),) if c != 768 else ((768, 384), (1152, 384)):
                    mine, theirs = (lt[0, rows, :], slt0[rows, :]) if lo < WIDE else (lt[core, rows, :], slt1[rows, :])
                    t = dot(mine, r1[core, :, lo : lo + n]) + dot(theirs, sr1[:, lo : lo + n])
                    sums[0][zh, x, :, :, :, lo : lo + n] = t.astype(BF16).reshape(4, 2, 16, n)
        over_blocks(body)

    fetched = {}

    def fetch(ref, i, n):
        if i < 8:
            b = i % 2
            fetched[i] = pltpu.make_async_copy(ref.at[i // 4, i % 4, :, :, :, pl.ds(0, n)], wbuf.at[b, :, :, :, pl.ds(0, n)], wsem.at[b])
            fetched[i].start()

    def second_norm_part(i):
        def run():
            if i == 0:
                need(1, 7, 2, 0, 11, 6, 12, 3, 9)
                fetch(g1, 0, FF)
                fetch(g1, 1, FF)
            if i < 8:
                fetched[i].wait()
                b = i % 2
                t = dot_nt(hg[0], wbuf[b, :, :, :, :2176].reshape(128, 2176)) + dot_nt(hg[1], wbuf[b, :, :, :, 2176:].reshape(128, 2176))
                fetch(g1, i + 2, FF)
            else:
                t = dot_nt(hg[0], v2[:, :2176]) + dot_nt(hg[1], v2[:, 2176:])
            dn[:, 128 * i : 128 * i + 128] = t
        return run

    def norm_back(values, gain):
        xhat, r = centred(values)
        e = dn[...]
        eg = e * gain
        m1 = jnp.sum(eg, axis=-1, keepdims=True) * (1.0 / REAL)
        m2 = jnp.sum(eg * xhat, axis=-1, keepdims=True) * (1.0 / REAL)
        back = jnp.where(iota((1, WIDE), 1) < REAL, r * (eg - m1 - xhat * m2), 0.0)
        return back, jnp.sum(e * xhat, axis=0, keepdims=True), jnp.sum(e, axis=0, keepdims=True)

    def total(t):
        return jnp.sum(t.astype(F32), axis=0, keepdims=True)

    def second_norm():
        back, gain_sum, shift_sum = norm_back(resid[...], vecs[5:6, :])
        t = cot[...].astype(F32) + back
        rgrad[...] = t
        low = t.astype(BF16)
        r1[1, :, WIDE:] = low
        small[4:5, :] = total(low)
        small[5:6, :] = gain_sum
        small[6:7, :] = shift_sum
        small[7:8, :] = total(cot[...])

    wo_copy = pltpu.make_async_copy(g0.at[:, :, :, :, :, pl.ds(3 * WIDE, WIDE)], wo, wsem.at[2])
    wo_copy.start()

    def attended_back():
        wo_copy.wait()
        low = r1[1, :, WIDE:]
        a = jnp.concatenate([dot_nt(low, wo[...].reshape(1024, WIDE)), dot_nt(low, v1[:, 3 * WIDE :])], axis=1).astype(BF16)
        gh[...] = dot_nt(a, perm[...]).astype(BF16)

    def attention_back(pair):
        def run():
            lanes = pl.ds(128 * pair, 128)
            q, k, v, g = qkv[0, :, lanes], qkv[1, :, lanes], qkv[2, :, lanes], gh[:, lanes]
            low_half = iota((1, 128), 1) < 64
            dq = jnp.zeros((TOK, 128), F32)
            dk, dv = dq, dq
            for half in range(2):
                mask = low_half if half == 0 else jnp.logical_not(low_half)
                pick = lambda t: jnp.where(mask, t, jnp.zeros_like(t))
                qh, kh, vh, gg = pick(q), pick(k), pick(v), pick(g)
                sc = dot_nt(q, kh) * 0.125 + bias[0]
                e = jnp.exp(sc - jnp.max(sc, axis=1, keepdims=True))
                p = e / jnp.sum(e, axis=1, keepdims=True)
                dp = dot_nt(g, vh)
                ds = (p * (dp - jnp.sum(p * dp, axis=1, keepdims=True))).astype(BF16)
                dq = dq + dot(ds, kh)
                sc = dot_nt(k, qh) * 0.125 + bias[1]
                e = jnp.exp(sc - jnp.max(sc, axis=0, keepdims=True))
                p = e / jnp.sum(e, axis=0, keepdims=True)
                dp = dot_nt(v, gg)
                ds = (p * (dp - jnp.sum(p * dp, axis=0, keepdims=True))).astype(BF16)
                dk = dk + dot(ds, qh)
                dv = dv + dot(p.astype(BF16), gg)
            lo = 128 * pair
            dq, dk, dv = (dq * 0.125).astype(BF16), (dk * 0.125).astype(BF16), dv.astype(BF16)
            r1[0, :, lo : lo + 128] = dq
            r1[0, :, WIDE + lo : WIDE + lo + 128] = dk
            r1[1, :, lo : lo + 128] = dv
            small[2:3, lo : lo + 128] = total(dq)
            small[3:4, lo : lo + 128] = total(dv)
        return run

    def give_first():
        give(6, r1.at[other], sr1)

    def first_norm_part(i):
        def run():
            if i == 0:
                fetch(g0, 0, 3 * WIDE)
                fetch(g0, 1, 3 * WIDE)
            if i < 8:
                fetched[i].wait()
                b = i % 2
                t = dot_nt(r1[0], wbuf[b, :, :, :, :2304].reshape(128, 2304)) + dot_nt(r1[1, :, :WIDE], wbuf[b, :, :, :, 2304:3456].reshape(128, WIDE))
                fetch(g0, i + 2, 3 * WIDE)
            else:
                t = dot_nt(r1[0], v1[:, :2304]) + dot_nt(r1[1, :, :WIDE], v1[:, 2304:3456])
            dn[:, 128 * i : 128 * i + 128] = t
        return run

    def first_norm():
        back, gain_sum, shift_sum = norm_back(tokens[...].astype(F32), vecs[0:1, :])
        rgrad[...] = rgrad[...] + back
        small[0:1, :] = gain_sum
        small[1:2, :] = shift_sum

    def natural_grad():
        t = rgrad[...]
        high = t.astype(BF16)
        t = t - high.astype(F32)
        mid = t.astype(BF16)
        low = (t - mid.astype(F32)).astype(BF16)
        grad[...] = dot_nt(high, perm[...]) + dot_nt(mid, perm[...]) + dot_nt(low, perm[...])

    def left_rows(t):
        def run():
            def put(i, values):
                left[i // 16, pl.ds(i % 16, 32, stride=16), :] = values

            tail = pl.ds(1024, 64)
            for j in range(9):
                lane = 512 * j + 128 * t
                rhs = r1[0, :, lane : lane + 128] if lane < 2304 else r1[1, :, lane - 2304 : lane - 2176]
                v = dot(lt[1 if lane >= 3 * WIDE else 0, tail, :], rhs)
                put(j, v[:32])
                put(9 + j, v[32:])
                if lane < FF:
                    rhs = hg[0, :, lane : lane + 128] if lane < 2176 else hg[1, :, lane - 2176 : lane - 2048]
                    v = dot(nst[tail, :], rhs)
                else:
                    v = jnp.zeros((64, 128), F32)
                put(18 + j, v[:32])
                put(27 + j, v[32:])
            for j in range(3):
                lane = 512 * j + 128 * t
                for b in range(2):
                    v = dot(actt[32 + b].reshape(128, TOK), cot[:, lane : lane + 128]) if lane < WIDE else jnp.zeros((128, 128), F32)
                    for i in range(4):
                        put(36 + 3 * (4 * b + i) + j, v[32 * i : 32 * i + 32])
            pick, own = dealt_pick()
            for i in range(2):
                v = small[4 * i + t : 4 * i + t + 1, :].astype(BF16)
                if i == 0 and t >= 2:
                    v = dot(v, perm[...]).astype(BF16)
                put(60 + i, dot_nt((own * v.astype(F32)).astype(BF16), pick))
            pick, own = hidden_pick(t)
            v = jnp.concatenate([total(hg[0]), total(hg[1])], axis=1)
            put(62, dot_nt((own * v).astype(BF16), pick))
            put(63, jnp.zeros((32, 128), F32))
            for zl in range(2):
                sums[3][:, :, :, zl, :, 128 * t : 128 * t + 128] = left[2 * zl + core].reshape(2, 4, 4, 16, 128).astype(BF16)
                pr[:, :, :, zl, :, 128 * t : 128 * t + 128] = left[2 * zl + other].reshape(2, 4, 4, 16, 128).astype(BF16)
        return run

    def give_left():
        give(7, pr, spr)

    def take_left():
        exchange[7].wait_recv()
        def body(zh, x, i):
            sums[3][zh, x] = (sums[3][zh, x].astype(F32) + spr[zh, x].astype(F32)).astype(BF16)
        over_blocks(body)

    C = lambda c, k: (lambda: comm(c, k))
    n2 = [second_norm_part(i) for i in range(9)]
    at_ = [attention_back(i) for i in range(9)]
    n1 = [first_norm_part(i) for i in range(9)]
    script = [down_weight, C(0, 0), up_weight, C(1, 0)] + n2 + [second_norm, C(0, 1), attended_back, C(1, 1)]
    script += at_[:3] + [C(0, 2)] + at_[3:6] + [C(1, 2)] + at_[6:] + [give_first, C(0, 3), C(1, 3)]
    script += [first_weight, C(2, 0)] + n1[:5] + [C(0, 4), C(1, 4)] + n1[5:] + [first_norm] + [left_rows(t) for t in range(4)] + [give_left]
    script += [C(2, 1), C(0, 5), C(1, 5), take_left, C(3, 0), natural_grad, C(2, 2), C(0, 6), C(1, 6), C(3, 1), C(2, 3), C(3, 2)]
    script += [C(2, 4), C(3, 3), C(2, 5), C(3, 4), C(2, 6), C(3, 5), C(3, 6), C(0, 7), C(1, 7), C(2, 7), C(3, 7)]
    for f in script:
        f()
    for c in local:
        c.wait()
    for c in pending:
        c.wait_send()
    for u in range(len(U)):
        for phase in range(3):
            sent(u, phase)


def backward_call(*ops):
    U = scatter_units()
    V, D, S = pltpu.VMEM, pltpu.SemaphoreType.DMA, jax.ShapeDtypeStruct
    here, vm = pl.BlockSpec(memory_space=pl.ANY), pl.BlockSpec(memory_space=pltpu.VMEM)
    scratch = [V((2, 4, 4, 2, 16, 2304), BF16), V((2, 4, 4, 2, 16, 2176), BF16), V((2, 4, 4, 2, 32, WIDE), BF16), V((2, 4, 4, 2, 16, 512), BF16)]
    scratch += [V((32, 2, 32, TOK), BF16), V((TOK, WIDE), BF16), V((WIDE, TOK), BF16), V((TOK, 2176), BF16), V((WIDE, TOK), BF16), V((WIDE, TOK), BF16)]
    scratch += [V((TOK, 2304), BF16), V((2, 4, 4, 2, 16, 512), BF16)]
    scratch += [V((2, 4, 2, 16, FF), BF16), V((2, 4, 4, 2, 16, WIDE), BF16), V((TOK, WIDE), F32), V((TOK, WIDE), F32), V((2, TOK, 2304), BF16)]
    scratch += [V((TOK, WIDE), BF16), V((4, 512, 128), F32), V((2, 4, 4, 2, 16, 512), BF16), V((8, WIDE), F32)]
    for w, g, c0, h0, h1 in U:
        for p in range(3):
            dims = block_dims(ORDERS[g][::-1], p)
            scratch += [V((3,) + dims + (ROWS[w], h0), BF16), V((3,) + dims + (ROWS[w], h1), BF16)]
    n = len(U)
    scratch += [D((n, 3, 2)), D((n, 3, 4)), D((8,)), D((8,)), D((n, 3)), D((n, 3)), D((n,)), D((3,))]
    scratch += [V(o.shape, o.dtype) for o in ops[2:]] + [D((13,))]
    return pl.pallas_call(
        backward_kernel,
        out_shape=(S((2, 16, 4608), BF16), S((2, 16, FF), BF16), S((2, 2, 32, WIDE), BF16), S((2, 2, 16, 512), BF16), S((TOK, WIDE), F32)),
        in_specs=[here] * 15,
        out_specs=(here,) * 4 + (vm,),
        scratch_shapes=scratch,
        compiler_params=pltpu.CompilerParams(collective_id=1, has_side_effects=True, vmem_limit_bytes=63 * 2**20),
    )(*ops)


def body(*args):
    pieces, tokens, cot, perm, turn, bias = prepare(*args)
    g0, g1, g2, g3, v1, v2, vecs, lt, nst, actt, qkv, resid, hg, layer_out = forward_call(*pieces, tokens, cot, perm, bias)
    both = jnp.stack([bias, bias.T])
    s0, s1, s2, s3, grad = backward_call(g0, g1, v1, v2, vecs, lt, nst, actt, qkv, resid, hg, tokens, cot, perm, both)
    left = s3.reshape(64, 512)
    first = jnp.concatenate([s0.reshape(32, 4608), left[:18].reshape(2, 4608)], axis=0)
    up_d = jnp.concatenate([s1.reshape(32, FF), left[18:36].reshape(2, 4608)[:, :FF]], axis=0)
    up_left = dot_nt(up_d[:, 4096:], turn).astype(BF16).reshape(34, 4, 64)
    up_d = widen(jnp.concatenate([up_d[:, :4096].reshape(34, 4, 1024), up_left], axis=2))
    down_d = jnp.concatenate([s2.reshape(4, 32, WIDE), left[36:60].reshape(4, 2, 1536)[:, :, :WIDE]], axis=1)
    stacked = jnp.concatenate([first[:, 3 * WIDE :], up_d.reshape(136, WIDE), down_d.reshape(136, WIDE)], axis=0)
    stacked = dot_nt(stacked, perm[:REAL])
    small = left[60:62].reshape(8, 128)[:, :34].astype(F32)
    units = left[62].reshape(4, 128)[:, :34].reshape(136).astype(F32)
    qkv_grad = first[:, : 3 * WIDE].reshape(34, 3, WIDE)[:, :, :REAL].reshape(34, 3 * REAL).astype(F32)
    return (
        layer_out[:, :REAL], grad[:, :REAL], small[0], small[1], qkv_grad, small[2], small[3], stacked[:34], small[4],
        small[5], small[6], stacked[34:170].reshape(34, FF), units, stacked[170:], small[7],
    )


def solution(mesh):
    ins, outs = specs()
    return jax.shard_map(body, mesh=mesh, in_specs=ins, out_specs=outs, check_vma=False)
```

```python
import jax
import jax.numpy as jnp
import ml_dtypes
import numpy as np
from jax import lax
from jax.experimental import pallas as pl
from jax.experimental.pallas import tpu as pltpu
from jax.sharding import PartitionSpec as P

MESH = pl.DeviceIdType.MESH
F32, BF16 = jnp.float32, jnp.bfloat16
AXES = "xyz"
ORDERS = ("xyz", "yzx", "zxy")
TOK = 160
WIDE = 1152
REAL = 1088
FF = 4352
epsilon = 1e-05
excluded = -1000000000.0
PER_STEP = 3
ROOT = 0.7978845608028654


def place():
    f = lax.axis_index("fsdp")
    r = lax.axis_index("rep")
    return dict(x=(f // 4) % 4, y=f % 4, z=(f // 16) * 2 + r // 2), r % 2


def device(at, core):
    z = at["z"]
    return ((z // 2) * 16 + at["x"] * 4 + at["y"], (z % 2) * 2 + core)


def moved(at, axis, step):
    return {**at, axis: lax.rem(at[axis] + step + 4, 4)}


def meet(devices):
    barrier = pltpu.get_barrier_semaphore()
    for d in devices:
        pl.semaphore_signal(barrier, inc=1, device_id=d, device_id_type=MESH)
    pl.semaphore_wait(barrier, len(devices))


def dot(a, b):
    return jnp.dot(a, b, preferred_element_type=F32)


def dot_nt(a, b):
    return lax.dot_general(a, b, (((1,), (1,)), ((), ())), preferred_element_type=F32)


def iota(shape, dim):
    return lax.broadcasted_iota(jnp.int32, shape, dim)


def eye(n):
    return jnp.where(iota((n, n), 0) == iota((n, n), 1), 1.0, 0.0).astype(BF16)


def dealt_pick():
    r, c = iota((128, WIDE), 0), iota((128, WIDE), 1)
    want = jnp.where(c < 1024, c & 31, jnp.where(c < REAL, 32 + ((c - 1024) >> 5), -1))
    s, c = iota((32, WIDE), 0), iota((32, WIDE), 1)
    owner = jnp.where(c < 1024, c >> 5, c & 31)
    return jnp.where(r == want, 1.0, 0.0).astype(BF16), jnp.where(s == owner, 1.0, 0.0)


def hidden_pick(k):
    r, c = iota((128, FF), 0), iota((128, FF), 1)
    want = jnp.where(c < 4096, c & 31, 32 + (((c - 4096) >> 5) & 1))
    s, c = iota((32, FF), 0), iota((32, FF), 1)
    d = c - 4096
    owner = jnp.where(c < 4096, c >> 5, 4 * (d & 31) + (d >> 6))
    return jnp.where(r == want, 1.0, 0.0).astype(BF16), jnp.where(4 * s + k == owner, 1.0, 0.0)


def centred(values):
    valid = iota((1, WIDE), 1) < REAL
    average = jnp.sum(values, axis=-1, keepdims=True) * (1.0 / REAL)
    c = jnp.where(valid, values - average, 0.0)
    r = lax.rsqrt(jnp.sum(c * c, axis=-1, keepdims=True) * (1.0 / REAL) + epsilon)
    return c * r, r


def gather_chunks():
    whole = [
        [(3, 0, 0, 16, 0, 256, 256)],
        [(0, 0, 0, 16, 0, 256, 256), (0, 1, 0, 16, 512, 512, 384), (0, 2, 0, 16, 1408, 512, 384)],
        [(1, 0, 0, 16, 0, 384, 256), (1, 1, 0, 16, 640, 384, 384), (1, 2, 0, 16, 1408, 384, 384)],
        [(2, g, 0, 32, 384 * g, 256, 128) for g in range(3)],
    ]
    parts = [
        [(3, 0, 0, 16, 0, 256, 256)],
        [(0, 0, 0, 16, 0, 128, 128), (0, 1, 0, 16, 512, 256, 256), (0, 2, 0, 16, 1408, 256, 256)],
        [(0, 0, 0, 16, 256, 128, 128), (0, 1, 0, 16, 1024, 256, 128), (0, 2, 0, 16, 1920, 256, 128)],
        [(1, 0, 0, 16, 0, 256, 128), (1, 1, 0, 16, 640, 256, 128), (1, 2, 0, 16, 1408, 256, 128)],
        [(1, 0, 0, 16, 384, 128, 128), (1, 1, 0, 16, 1024, 256, 128), (1, 2, 0, 16, 1792, 256, 128)],
        [(2, g, 0, 16, 384 * g, 256, 128) for g in range(3)],
        [(2, g, 16, 16, 384 * g, 256, 128) for g in range(3)],
    ]
    return whole, parts


HALF = (2304, 2176)
PAIR = "pair"


def slot(ref, w, idx, core, rows, cols):
    z = idx["z"]
    every = slice(None)
    if z is None or z is PAIR:
        zh, zl = (every if z is None else 0), every
    else:
        zh, zl = z // 2, lax.rem(z, 2)
    x, y = (every if idx[a] is None else pl.ds(0, 2) if idx[a] is PAIR else idx[a] for a in "xy")
    if w < 2:
        return ref.at[zh, x, y, zl, :, pl.ds(pl.multiple_of(core * HALF[w] + cols[0], 128), cols[1])]
    return ref.at[zh, x, y, zl, core, pl.ds(rows[0], rows[1]), pl.ds(cols[0], cols[1])]


def forward_kernel(
    p0, p1, p2, p3, tokens_in, cot_in, perm_in, bias_in,
    g0, g1, g2, g3, out_v1, out_v2, out_vecs, out_lt, out_nst, out_actt, out_qkv, out_resid, out_hg, out,
    w1, w2, w3, rest, unpacked, v3, upb, nf, att, attd, act, gp, v1, v2, vecs, lt, nst, actt, qkv, resid, ns, hg,
    tokens, cot, perm, bias, send, recv, ssend, srecv, lsem, wsem, osem, isem,
):
    at, core = place()
    me = device(at, core)
    sibling = device(at, 1 - core)
    near = {(a, s): device(moved(at, a, s), core) for a in AXES for s in (1, -1)}
    across_ring = {a: device(moved(at, a, 2), core) for a in AXES}
    meet(list(near.values()) + list(across_ring.values()) + [sibling])
    ins, outs = (p0, p1, p2, p3), (g0, g1, g2, g3)
    whole, parts = gather_chunks()
    U = [u for c in whole + parts for u in c]
    ids, n = [], 0
    for c in whole + parts:
        ids.append(list(range(n, n + len(c))))
        n += len(c)
    whole_ids, part_ids = ids[: len(whole)], ids[len(whole) :]
    whole_ids_flat = [u for c in whole_ids for u in c]
    started = []

    def block(u, phase, pos):
        order = ORDERS[U[u][1]]
        idx = dict(at)
        for a in order[:phase]:
            idx[a] = None
        idx[order[phase]] = pos
        return idx

    many = len(whole_ids_flat)

    def number(u, phase, b):
        return 4 * u + 2 * phase + b if u < many else 4 * many + 2 * (u - many) + b

    def ref_of(u, idx, cols, c=None):
        w, g, r0, nr = U[u][:4]
        return slot(outs[w], w, idx, core if c is None else c, (r0, nr), cols)

    def remote(src, dst, dev, s, r):
        return pltpu.make_async_remote_copy(src_ref=src, dst_ref=dst, send_sem=s, recv_sem=r, device_id=dev, device_id_type=MESH)

    def ring(u, phase, b, ref, dev, src=None):
        i = number(u, phase, b)
        remote(ref if src is None else src, ref, dev, send.at[i], recv.at[i]).start()

    def spots(u, phase):
        w, g, r0, nr, c0, h0, h1 = U[u]
        axis = ORDERS[g][phase]
        pos = at[axis]
        return axis, pos, [lax.rem(pos + i, 4) for i in (1, 3, 2)], (c0, h0 + h1), (c0, h0), (c0 + h0, h1)

    def go(u, k):
        w, g, r0, nr, c0, h0, h1 = U[u]
        phase, b = divmod(k, 2)
        axis, pos, (pp, pm, po), full, A, B = spots(u, phase)
        plus, minus = near[axis, 1], near[axis, -1]
        if b == 0:
            src = ins[w].at[pl.ds(r0, nr), pl.ds(c0, h0 + h1)] if phase == 0 else None
            own = ref_of(u, block(u, phase, pos), full)
            ring(u, phase, 0, own, plus, src)
            ring(u, phase, 0, own, minus, src)
            if phase == 0:
                ring(u, 0, 1, own, across_ring[axis], src)
                started.append((u, 0, 1))
        else:
            ring(u, phase, 1, ref_of(u, block(u, phase, pm), A), plus)
            ring(u, phase, 1, ref_of(u, block(u, phase, pp), B), minus)
        started.append((u, phase, b))

    def in_flight(u, phase, b):
        axis, pos, others, full, A, B = spots(u, phase)
        ref = ref_of(u, block(u, phase, pos if b else PAIR), full)
        i = number(u, phase, b)
        return remote(ref, ref, me, send.at[i], recv.at[i])

    def arrive(u, k):
        in_flight(u, *divmod(k, 2)).wait_recv()

    def across(u, j):
        axis, pos, others, full, A, B = spots(u, 2)
        ref = ref_of(u, block(u, 2, ([pos] + others)[j]), full)
        remote(ref, ref, sibling, ssend.at[u - many], srecv.at[u - many]).start()

    def all_across(u, c):
        axis, pos, others, full, A, B = spots(u, 2)
        ref = ref_of(u, dict(x=None, y=None, z=None), full, c)
        return remote(ref, ref, me, ssend.at[u - many], srecv.at[u - many])

    def arrive_across(u):
        all_across(u, 1 - core).wait_recv()

    entries = []
    for i, (a, b) in enumerate(((perm_in, perm), (tokens_in, tokens), (bias_in, bias), (cot_in, cot))):
        c = pltpu.make_async_copy(a, b, isem.at[i])
        c.start()
        entries.append(c)
    own_copies = []
    for w in range(4):
        cols = (0, (2304, 2176, WIDE, 512)[w])
        rows = (0, (16, 16, 32, 16)[w])
        c = pltpu.make_async_copy(ins[w], slot(outs[w], w, at, core, rows, cols), lsem.at[w])
        c.start()
        own_copies.append(c)

    def early(c, k):
        def run():
            for u in whole_ids[c]:
                if k == 2:
                    arrive(u, 0)
                if k > 0:
                    arrive(u, k - 1)
                if k < 4:
                    go(u, k)
        return run

    def third(c):
        def run():
            for u in part_ids[c]:
                go(u, 4)
            for u in part_ids[c]:
                across(u, 0)
        return run

    def onward(c):
        def run():
            for u in part_ids[c]:
                arrive(u, 4)
                go(u, 5)
            for u in part_ids[c]:
                across(u, 1)
                across(u, 2)
        return run

    def last(c):
        def run():
            for u in part_ids[c]:
                arrive(u, 5)
                across(u, 3)
        return run

    loads = {}
    written = []

    def write(src, dst):
        def run():
            c = pltpu.make_async_copy(src, dst, osem.at[len(written)])
            c.start()
            written.append(c)
        return run


    def load(name, src, dst, i):
        loads[name] = pltpu.make_async_copy(src, dst, wsem.at[i])
        loads[name].start()

    def landed(c):
        for u in part_ids[c]:
            arrive_across(u)

    def weight(ref, lo, n):
        return ref[:, :, :, :, :, lo : lo + n].reshape(1024, n)

    def row(i):
        return vecs[i : i + 1, :]

    def stage_rest():
        for c in entries:
            c.wait()
        landed(0)
        load("rest", g3, rest, 3)
        loads["rest"].wait()
        for q in range(4):
            for t in range(4):
                piece = rest[:, :, :, q // 2, q % 2, :, 128 * t : 128 * t + 128].astype(F32)
                unpacked[t, q] = piece.reshape(512, 128)

    def gathered_row(i, t):
        return unpacked[t, i // 16, pl.ds(i % 16, 32, stride=16), :]

    def stage_vectors():
        pick, own = dealt_pick()
        rows = []
        for i in range(8):
            b = gathered_row(60 + i // 4, i % 4).astype(BF16)
            rows.append(jnp.sum(own * dot(b, pick), axis=0, keepdims=True))
        all_rows = jnp.concatenate(rows, axis=0)
        natural = dot_nt(all_rows.astype(BF16), perm[...])
        vecs[...] = jnp.concatenate([all_rows[:2], natural[2:4], all_rows[4:]], axis=0)

    def stage_units(k):
        def run():
            pick, own = hidden_pick(k)
            b = gathered_row(62, k).astype(BF16)
            t = jnp.sum(own * dot(b, pick), axis=0, keepdims=True)
            upb[...] = t if k == 0 else upb[...] + t
        return run

    def stage_left(w):
        def run():
            if w < 2:
                dst = (v1, v2)[w]
                for r in range(2):
                    for j in range(9):
                        for t in range(4):
                            lane = 512 * j + 128 * t
                            if lane < dst.shape[1]:
                                dst[32 * r : 32 * r + 32, lane : lane + 128] = gathered_row(18 * w + 9 * r + j, t).astype(BF16)
                dst[64:, :] = jnp.zeros((64, dst.shape[1]), BF16)
            else:
                for b in range(8):
                    for j in range(3):
                        for t in range(4):
                            lane = 512 * j + 128 * t
                            if lane < WIDE:
                                v3[32 * b : 32 * b + 32, lane : lane + 128] = gathered_row(36 + 3 * b + j, t).astype(BF16)
        return run

    def flipped(ref):
        parts = []
        for c in range(0, WIDE, 256):
            n = min(256, WIDE - c)
            parts.append((c, n, dot_nt(eye(n), ref[:, c : c + n]).astype(BF16)))
        return parts

    def stage_norm():
        xhat, r = centred(tokens[...].astype(F32))
        nf[...] = (xhat * row(0) + row(1)).astype(BF16)
        for c, n, t in flipped(nf):
            lt[0, c : c + n, :] = t

    def stage_load1():
        landed(1)
        landed(2)
        load("w1", g0, w1, 0)

    def stage_qkv(i):
        def run():
            if i == 0:
                loads["w1"].wait()
            for c in (0, 384, 768):
                lo = WIDE * i + c
                t = dot(nf[:, :1024], weight(w1, lo, 384)) + dot(nf[:, 1024:], v1[:, lo : lo + 384])
                if i != 1:
                    t = t + vecs[2 + i // 2 : 3 + i // 2, c : c + 384]
                qkv[i, :, c : c + 384] = t.astype(BF16)
        return run

    def stage_attention(pair):
        def run():
            lanes = pl.ds(128 * pair, 128)
            q, k, v = qkv[0, :, lanes], qkv[1, :, lanes], qkv[2, :, lanes]
            low_half = iota((1, 128), 1) < 64
            total = jnp.zeros((TOK, 128), F32)
            for half in range(2):
                mask = low_half if half == 0 else jnp.logical_not(low_half)
                pick = lambda t: jnp.where(mask, t, jnp.zeros_like(t))
                s = dot_nt(q, pick(k)) * 0.125 + bias[...]
                e = jnp.exp(s - jnp.max(s, axis=-1, keepdims=True))
                p = e / jnp.sum(e, axis=-1, keepdims=True)
                total = total + dot(p.astype(BF16), pick(v))
            att[:, lanes] = total.astype(BF16)
        return run

    def stage_out():
        attd[...] = dot(att[...], perm[...]).astype(BF16)
        for c in (0, 384, 768):
            lo = 3 * WIDE + c
            t = dot(attd[:, :1024], weight(w1, lo, 384)) + dot(attd[:, 1024:], v1[:, lo : lo + 384])
            resid[:, c : c + 384] = tokens[:, c : c + 384].astype(F32) + t + vecs[4:5, c : c + 384]
        for c, n, t in flipped(attd):
            lt[1, c : c + n, :] = t

    def stage_norm2():
        xhat, r = centred(resid[...])
        ns[...] = (xhat * row(5) + row(6)).astype(BF16)
        for c, n, t in flipped(ns):
            nst[c : c + n, :] = t

    def stage_load2():
        landed(3)
        landed(4)
        load("w2", g1, w2, 1)

    def stage_up(half, c, n):
        def run():
            if half == 0 and c == 0:
                loads["w2"].wait()
            lo = 2176 * half + c
            u = dot(ns[:, :1024], weight(w2, lo, n)) + dot(ns[:, 1024:], v2[:, lo : lo + n]) + upb[:, lo : lo + n]
            t = jnp.tanh(ROOT * (u + 0.044715 * u * u * u))
            a = (0.5 * u * (1.0 + t)).astype(BF16)
            act[:, lo : lo + n] = a
            gp[:, lo : lo + n] = 0.5 * (1.0 + t) + 0.5 * u * (1.0 - t * t) * (ROOT * (1.0 + 3 * 0.044715 * u * u))
            for j in range(0, n, 128):
                f = lo + j
                flip = dot_nt(eye(128), a[:, j : j + 128]).astype(BF16)
                if f < 4096:
                    actt[f // 128] = flip.reshape(2, 2, 32, TOK)
                else:
                    actt[f // 128] = flip.reshape(2, 2, 32, TOK)
        return run

    def stage_load3(i):
        def run():
            landed(5 + i)
            r = pl.ds(16 * i, 16)
            load(f"w3{i}", g2.at[:, :, :, :, :, r, :], w3.at[:, :, :, :, :, r, :], 2 + 2 * i)
        return run

    def stage_loaded3():
        loads["w30"].wait()
        loads["w31"].wait()

    def stage_down(c):
        def run():
            t = dot(act[:, :4096], w3[:, :, :, :, :, :, c : c + 384].reshape(4096, 384))
            t = t + dot(act[:, 4096:], v3[:, c : c + 384])
            attd[:, c : c + 384] = (resid[:, c : c + 384] + t + vecs[7:8, c : c + 384]).astype(BF16)
        return run

    def stage_result():
        out[...] = dot_nt(attd[...], perm[...]).astype(BF16)

    def stage_hidden(zh, x):
        def run():
            f = (zh * 4 + x) * 512
            d = dot_nt(cot[...], w3[zh, x].reshape(512, WIDE))
            g = (d * gp[:, f : f + 512]).astype(BF16)
            put_hidden(f, 512, g)
        return run

    def put_hidden(f, n, g):
        if f + n <= 2176:
            hg[0, :, f : f + n] = g
        elif f >= 2176:
            hg[1, :, f - 2176 : f - 2176 + n] = g
        else:
            m = 2176 - f
            hg[0, :, f:2176] = g[:, :m]
            hg[1, :, : n - m] = g[:, m:]

    def stage_hidden_left():
        d = dot_nt(cot[...], v3[...])
        put_hidden(4096, 256, (d * gp[:, 4096:]).astype(BF16))

    ups = [stage_up(h, c, n) for h in range(2) for c, n in ((0, 512), (512, 512), (1024, 512), (1536, 640))]
    lefts = [stage_left(w) for w in range(3)]
    work = {
        0: [stage_rest, stage_vectors] + [stage_units(k) for k in range(4)] + [stage_norm] + lefts + [write(v1, out_v1), write(v2, out_v2), write(vecs, out_vecs)],
        2: [stage_load1] + [stage_qkv(i) for i in range(3)] + [write(qkv, out_qkv)] + [stage_attention(i) for i in range(9)] + [stage_out, write(resid, out_resid), write(lt, out_lt), stage_norm2, write(nst, out_nst)],
        4: [stage_load2] + ups + [write(actt, out_actt)],
        5: [stage_load3(0)],
        6: [stage_load3(1), stage_loaded3] + [stage_hidden(zh, x) for zh in range(2) for x in range(4)] + [stage_hidden_left, write(hg, out_hg)] + [stage_down(c) for c in (0, 384, 768)] + [stage_result],
    }
    queue = []

    def compute(n):
        for _ in range(min(n, len(queue))):
            queue.pop(0)()

    script = "e00 e10 e20 e30 own e02 e12 e22 e32 e03 e13 e23 e33 "
    script += "e04 t0 e14 t1 t2 e24 e34 t3 o0 o1 t4 o2 - t5 l0 - l1 - l2 - o3 - t6 - o4 - - l3 - l4 - o5 - - o6 - l5 - l6"
    waiting = []
    for word in script.split():
        if word == "own":
            for c in own_copies:
                c.wait()
        elif word == "-":
            compute(PER_STEP)
            for w in waiting:
                queue.extend(work.get(w, []))
            waiting = []
        elif word[0] == "e":
            early(int(word[1]), int(word[2]))()
        else:
            {"t": third, "o": onward, "l": last}[word[0]](int(word[1]))()
            if word[0] == "l":
                waiting.append(int(word[1]))
    for w in waiting:
        queue.extend(work.get(w, []))
    compute(len(queue))
    for c in written:
        c.wait()
    for u, phase, b in started:
        in_flight(u, phase, b).wait_send()
    for u in [u for c in part_ids for u in c]:
        all_across(u, core).wait_send()


def forward_call(p0, p1, p2, p3, tokens, cot, perm, bias):
    whole, parts = gather_chunks()
    n, m = sum(len(c) for c in whole), sum(len(c) for c in parts)
    D, V = pltpu.SemaphoreType.DMA, pltpu.VMEM
    here, vm = pl.BlockSpec(memory_space=pl.ANY), pl.BlockSpec(memory_space=pltpu.VMEM)
    S = jax.ShapeDtypeStruct
    kept = [
        ((128, 4608), BF16), ((128, FF), BF16), ((8, WIDE), F32), ((2, WIDE, TOK), BF16), ((WIDE, TOK), BF16),
        ((34, 2, 2, 32, TOK), BF16), ((3, TOK, WIDE), BF16), ((TOK, WIDE), F32), ((2, TOK, 2176), BF16),
    ]
    gathered = [(2, 4, 4, 2, 16, 4608), (2, 4, 4, 2, 16, FF), (2, 4, 4, 2, 2, 32, WIDE), (2, 4, 4, 2, 2, 16, 512)]
    scratch = [V(shape, BF16) for shape in gathered]
    scratch += [
        V((4, 4, 512, 128), F32), V((256, WIDE), BF16), V((1, FF), F32),
        V((TOK, WIDE), BF16), V((TOK, WIDE), BF16), V((TOK, WIDE), BF16), V((TOK, FF), BF16), V((TOK, FF), F32),
    ]
    scratch += [V(*k) for k in kept[:8]] + [V((TOK, WIDE), BF16), V(*kept[8])]
    scratch += [V((TOK, WIDE), BF16), V((TOK, WIDE), BF16), V((WIDE, WIDE), BF16), V((TOK, TOK), F32)]
    scratch += [D((4 * n + 2 * m,)), D((4 * n + 2 * m,)), D((m,)), D((m,)), D((4,)), D((5,)), D((len(kept),)), D((4,))]
    return pl.pallas_call(
        forward_kernel,
        out_shape=tuple(S(shape, BF16) for shape in gathered) + tuple(S(*k) for k in kept) + (S((TOK, WIDE), BF16),),
        in_specs=[here] * 8,
        out_specs=(here,) * 13 + (vm,),
        scratch_shapes=scratch,
        compiler_params=pltpu.CompilerParams(collective_id=0, has_side_effects=True, vmem_limit_bytes=62 * 2**20),
    )(p0, p1, p2, p3, tokens, cot, perm, bias)


def dealt():
    natural = np.arange(WIDE)
    block, row = natural // 34, natural % 34
    target = np.where(row < 32, block * 32 + row, 1024 + (row - 32) * 32 + block)
    target = jnp.asarray(np.where(natural < REAL, target, -1).astype(np.int32))
    return (target[:, None] == lax.broadcasted_iota(jnp.int32, (WIDE, WIDE), 1)).astype(BF16)


def hidden_left():
    a = np.arange(256)
    j, r, s, q = a // 64, (a // 32) % 2, (a // 4) % 8, a % 4
    target = jnp.asarray(((q * 2 + r) * 32 + j * 8 + s).astype(np.int32))
    return (target[:, None] == lax.broadcasted_iota(jnp.int32, (256, 256), 1)).astype(BF16)


def causal_segments(seq_lengths, count):
    ends = jnp.cumsum(seq_lengths)
    position = jnp.arange(count, dtype=jnp.int32)
    segment = jnp.sum((position[:, None] >= ends[None, :]).astype(jnp.int32), axis=1)
    return (segment[:, None] == segment[None, :]) & (position[:, None] >= position[None, :])


def column_sum(rows):
    return jnp.sum(rows.astype(F32), axis=0)


def widen(t, n=WIDE):
    return jnp.pad(t, [(0, 0)] * (t.ndim - 1) + [(0, n - t.shape[-1])])


def own_pieces(q, core, moved_rows, left, vectors, qkv_weight):
    out_d, up_d, down_d = moved_rows[:34], moved_rows[34:170].reshape(34, 4, WIDE), moved_rows[170:306].reshape(4, 34, WIDE)
    up_left = dot(up_d[:, :, 1024:REAL].reshape(34, 256), left).astype(BF16)
    up_d = jnp.concatenate([up_d[:, :, :1024].reshape(34, 4096), up_left], axis=1)
    first = jnp.concatenate([widen(qkv_weight.reshape(34, 3, REAL)).reshape(34, 3456), out_d], axis=1)
    zl = q // 2
    p0 = lax.dynamic_slice(first, (zl * 16, core * 2304), (16, 2304))
    p1 = lax.dynamic_slice(up_d, (zl * 16, core * 2176), (16, 2176))
    p2 = lax.dynamic_slice(down_d, (q, 0, 0), (1, 32, WIDE))[0]
    bias = jnp.concatenate([widen(jnp.stack(vectors[:8]), 128).reshape(2, 512), widen(vectors[8].reshape(4, 34), 128).reshape(1, 512)], axis=0)
    rest = jnp.concatenate(
        [first[32:].reshape(18, 512), widen(up_d[32:], 4608).reshape(18, 512), widen(down_d[:, 32:], 1536).reshape(24, 512), bias, jnp.zeros((1, 512), BF16)],
        axis=0,
    )
    p3 = lax.dynamic_slice(rest, (q * 16, 0), (16, 512))
    return p0, p1, p2, p3


def specs():
    t, m, v = P(("fsdp", "rep"), None), P("fsdp", None), P("fsdp")
    return (t, t, t, v, v, m, v, v, m, v, v, v, m, v, m, v), (t, t, v, v, m, v, v, m, v, v, v, m, v, m, v)


def prepare(tokens, lengths, cotangent, attn_gain, attn_shift, qkv_weight, query_bias, value_bias, out_weight, out_bias, mlp_gain, mlp_shift, up_weight, up_bias, down_weight, down_bias):
    rank = lax.axis_index("rep")
    core = rank % 2
    perm = dealt()
    left = hidden_left()
    vectors = [attn_gain, attn_shift, query_bias, value_bias, out_bias, mlp_gain, mlp_shift, down_bias, up_bias]
    stacked = jnp.concatenate([out_weight, up_weight.reshape(136, REAL), down_weight, jnp.zeros((14, REAL), BF16), tokens, cotangent], axis=0)
    stacked = dot(stacked, perm[:REAL]).astype(BF16)
    pieces = own_pieces(rank, core, stacked, left, vectors, qkv_weight)
    bias = jnp.where(causal_segments(lengths[0], TOK), 0.0, excluded).astype(F32)
    return pieces, stacked[320:480], stacked[480:640], perm, left, bias


def scatter_units():
    out = [(2, g, 384 * g, 256, 128) for g in range(3)]
    out += [(1, 0, 0, 384, 256), (1, 1, 640, 384, 384), (1, 2, 1408, 384, 384)]
    out += [(0, 0, 0, 256, 256), (0, 1, 512, 512, 384), (0, 2, 1408, 512, 384)]
    return out + [(3, 0, 0, 256, 256)]


ROWS = (16, 16, 32, 16)
CHUNK_OF = {2: 0, 1: 1, 0: 2, 3: 3}


def block_dims(order, phase):
    free = order[phase + 1 :]
    dims = []
    if "z" in free:
        dims.append(2)
    if "x" in free:
        dims.append(4)
    if "y" in free:
        dims.append(4)
    if "z" in free:
        dims.append(2)
    return tuple(dims)


def part(ref, idx, cols):
    every = slice(None)
    z = idx["z"]
    zh, zl = (every, every) if z is None else (z // 2, lax.rem(z, 2))
    x = every if idx["x"] is None else idx["x"]
    y = every if idx["y"] is None else idx["y"]
    return ref.at[zh, x, y, zl, :, pl.ds(cols[0], cols[1])]


def backward_kernel(
    g0, g1, *rest,
):
    given, (o0, o1, o2, o3, grad), scratch = rest[:13], rest[13:18], rest[18:]
    U = scatter_units()
    at, core = place()
    other = 1 - core
    me = device(at, core)
    sibling = device(at, other)
    partner_at = {**at, "z": at["z"] + 1 - 2 * lax.rem(at["z"], 2)}
    partner, diagonal = device(partner_at, core), device(partner_at, other)
    near = {(a, s): device(moved(at, a, s), core) for a in AXES for s in (1, -1)}
    s = list(scratch)
    held, isem = s[-14:-1], s[-1]
    del s[-14:]
    v1, v2, vecs, lt, nst, actt, qkv, resid, hg, tokens, cot, perm, bias = held
    lt_in, nst_in, actt_in, hg_in, cot_in = given[3], given[4], given[5], given[8], given[10]
    sums = s[:4]
    sactt, scot, snst, shg, slt0, slt1, sr1, spr = s[4:12]
    wbuf, wo, dn, rgrad, r1, gh, left, pr, small = s[12:21]
    del s[:21]
    bufs = {}
    for u in range(len(U)):
        for p in range(3):
            bufs[u, p] = s[:2]
            del s[:2]
    send, recv, xsend, xrecv, rsend, rrecv, lsem, wsem = s
    across_ring = {a: device(moved(at, a, 2), core) for a in AXES}
    meet(list(near.values()) + list(across_ring.values()) + [sibling, diagonal])
    pending = []
    exchange = {}

    def give(i, src, dst):
        c = pltpu.make_async_remote_copy(src_ref=src, dst_ref=dst, send_sem=xsend.at[i], recv_sem=xrecv.at[i], device_id=sibling, device_id_type=MESH)
        c.start()
        pending.append(c)
        exchange[i] = c

    loads = {}
    for i in (5, 10, 4, 8, 1, 7, 2, 0, 11, 6, 12, 3, 9):
        loads[i] = pltpu.make_async_copy(given[i], held[i], isem.at[i])
    for i in (5, 10):
        loads[i].start()
    give(0, actt_in.at[pl.ds(0, 32), :, other], sactt)
    give(1, cot_in, scot)
    give(2, nst_in, snst)
    give(3, hg_in.at[other], shg)
    for i in (4, 8, 1, 7, 2, 0, 11, 6, 12, 3, 9):
        loads[i].start()
    give(4, lt_in.at[0], slt0)
    give(5, lt_in.at[other], slt1)

    def need(*which):
        for i in which:
            loads[i].wait()

    def block(u, phase, pos):
        order = ORDERS[U[u][1]][::-1]
        idx = {a: at[a] for a in AXES}
        idx[order[phase]] = pos
        for a in order[phase + 1 :]:
            idx[a] = None
        return idx

    def info(u, phase):
        w, g, c0, h0, h1 = U[u]
        axis = ORDERS[g][::-1][phase]
        pos = at[axis]
        pp, pm, po = (lax.rem(pos + i, 4) for i in (1, 3, 2))
        return w, (c0, h0), (c0 + h0, h1), near[axis, 1], near[axis, -1], pos, pp, pm, po

    def copies(u, phase):
        w, A, B, plus, minus, pos, pp, pm, po = info(u, phase)
        P_ = sums[w]
        ba, bb = bufs[u, phase]
        blk = lambda p, cols: part(P_, block(u, phase, p), cols)
        far = across_ring[ORDERS[U[u][1]][::-1][phase]] if phase == 2 else None
        plan = [
            (blk(po, A), ba.at[0], far or plus), (blk(po, B), bb.at[0], far or minus), (blk(pp, B), bb.at[1], plus),
            (blk(pm, A), ba.at[1], minus), (blk(pp, A), ba.at[2], plus), (blk(pm, B), bb.at[2], minus),
        ]
        first = (1, 0, 0, 1, 1, 0)
        land = (0, 1, 3, 2, 2, 3)
        return [
            pltpu.make_async_remote_copy(src_ref=a, dst_ref=b, send_sem=send.at[u, phase, first[i]], recv_sem=recv.at[u, phase, land[i]], device_id=d, device_id_type=MESH)
            for i, (a, b, d) in enumerate(plan)
        ]

    def landed(u, phase, i):
        ref = bufs[u, phase][i].at[pl.ds(1, 2)]
        pltpu.make_async_remote_copy(src_ref=ref, dst_ref=ref, send_sem=send.at[u, phase, 0], recv_sem=recv.at[u, phase, 2 + i], device_id=me, device_id_type=MESH).wait_recv()

    def sent(u, phase):
        for i in range(2):
            ref = bufs[u, phase][i]
            pltpu.make_async_remote_copy(src_ref=ref, dst_ref=ref, send_sem=send.at[u, phase, 1 - i], recv_sem=recv.at[u, phase, i], device_id=me, device_id_type=MESH).wait_send()

    live = {}

    def step_a(u, phase):
        cs = live[u, phase] = copies(u, phase)
        for c in cs if phase == 2 else cs[:4]:
            c.start()

    def add(ref, *terms):
        t = ref[...].astype(F32)
        for o in terms:
            t = t + o[...].astype(F32)
        ref[...] = t.astype(BF16)

    def step_b(u, phase):
        w, A, B, plus, minus, pos, pp, pm, po = info(u, phase)
        cs = live[u, phase]
        ba, bb = bufs[u, phase]
        cs[0].wait_recv()
        add(part(sums[w], block(u, phase, pp), A), ba.at[0])
        cs[4].start()
        cs[1].wait_recv()
        add(part(sums[w], block(u, phase, pm), B), bb.at[0])
        cs[5].start()

    def step_c(u, phase):
        w, A, B, plus, minus, pos, pp, pm, po = info(u, phase)
        cs = live[u, phase]
        ba, bb = bufs[u, phase]
        far = 0 if phase == 2 else 1
        if phase == 2:
            cs[0].wait_recv()
            cs[1].wait_recv()
        landed(u, phase, 0)
        add(part(sums[w], block(u, phase, pos), A), *[ba.at[i] for i in range(far, 3)])
        landed(u, phase, 1)
        add(part(sums[w], block(u, phase, pos), B), *[bb.at[i] for i in range(far, 3)])

    outs = (o0, o1, o2, o3)

    def out_part(w, zl, c, cols):
        if w < 2:
            return outs[w].at[zl, :, pl.ds(pl.multiple_of(c * HALF[w] + cols[0], 128), cols[1])]
        return outs[w].at[zl, c, :, pl.ds(cols[0], cols[1])]

    local = []

    def share(u):
        w, g, c0, h0, h1 = U[u]
        src = part(sums[w], at, (c0, h0 + h1))
        dst = out_part(w, lax.rem(at["z"], 2), core, (c0, h0 + h1))
        c = pltpu.make_async_copy(src, dst, lsem.at[u])
        c.start()
        local.append(c)
        for i, dev in enumerate((sibling, partner, diagonal)):
            c = pltpu.make_async_remote_copy(src_ref=src, dst_ref=dst, send_sem=rsend.at[u, i], recv_sem=rrecv.at[u, i], device_id=dev, device_id_type=MESH)
            c.start()
            pending.append(c)

    def share_wait(u):
        w, g, c0, h0, h1 = U[u]
        zl = lax.rem(at["z"], 2)
        src = part(sums[w], at, (c0, h0 + h1))
        for i, (z, c) in enumerate(((zl, other), (1 - zl, core), (1 - zl, other))):
            pltpu.make_async_remote_copy(
                src_ref=src, dst_ref=out_part(w, z, c, (c0, h0 + h1)), send_sem=rsend.at[u, i], recv_sem=rrecv.at[u, i], device_id=me, device_id_type=MESH
            ).wait_recv()

    chunks = [[u for u in range(len(U)) if CHUNK_OF[U[u][0]] == c] for c in range(4)]

    def comm(c, k):
        for u in chunks[c]:
            if k == 0:
                step_a(u, 0)
            elif k in (1, 3):
                step_b(u, k // 2)
            elif k == 5:
                continue
            elif k in (2, 4):
                step_c(u, k // 2 - 1)
                step_a(u, k // 2)
            elif k == 6:
                step_c(u, 2)
                share(u)
            else:
                share_wait(u)

    def over_blocks(body):
        def step(i, carry):
            body(i // 4, lax.rem(i, 4), i)
            return carry
        lax.fori_loop(0, 8, step, 0)

    def down_weight():
        need(5, 10)
        exchange[0].wait_recv()
        exchange[1].wait_recv()
        def body(zh, x, i):
            mine = actt[pl.ds(4 * i, 4), :, core].reshape(256, TOK)
            theirs = sactt[pl.ds(4 * i, 4)].reshape(256, TOK)
            for c in (0, 384, 768):
                t = dot(mine, cot[:, c : c + 384]) + dot(theirs, scot[:, c : c + 384])
                sums[2][zh, x, :, :, :, c : c + 384] = t.astype(BF16).reshape(4, 2, 32, 384)
        over_blocks(body)

    def up_weight():
        need(4, 8)
        exchange[2].wait_recv()
        exchange[3].wait_recv()
        def body(zh, x, i):
            rows = pl.ds(pl.multiple_of(128 * i, 128), 128)
            mine, theirs = nst[rows, :], snst[rows, :]
            for c, n in ((0, 768), (768, 768), (1536, 640)):
                t = dot(mine, hg[core, :, c : c + n]) + dot(theirs, shg[:, c : c + n])
                sums[1][zh, x, :, :, :, c : c + n] = t.astype(BF16).reshape(4, 2, 16, n)
        over_blocks(body)

    def first_weight():
        for i in (4, 5, 6):
            exchange[i].wait_recv()
        def body(zh, x, i):
            rows = pl.ds(pl.multiple_of(128 * i, 128), 128)
            for c in (0, 768, 1536):
                for lo, n in ((c, 768),) if c != 768 else ((768, 384), (1152, 384)):
                    mine, theirs = (lt[0, rows, :], slt0[rows, :]) if lo < WIDE else (lt[core, rows, :], slt1[rows, :])
                    t = dot(mine, r1[core, :, lo : lo + n]) + dot(theirs, sr1[:, lo : lo + n])
                    sums[0][zh, x, :, :, :, lo : lo + n] = t.astype(BF16).reshape(4, 2, 16, n)
        over_blocks(body)

    fetched = {}

    def fetch(ref, i, n):
        if i < 8:
            b = i % 2
            fetched[i] = pltpu.make_async_copy(ref.at[i // 4, i % 4, :, :, :, pl.ds(0, n)], wbuf.at[b, :, :, :, pl.ds(0, n)], wsem.at[b])
            fetched[i].start()

    def second_norm_part(i):
        def run():
            if i == 0:
                need(1, 7, 2, 0, 11, 6, 12, 3, 9)
                fetch(g1, 0, FF)
                fetch(g1, 1, FF)
            if i < 8:
                fetched[i].wait()
                b = i % 2
                t = dot_nt(hg[0], wbuf[b, :, :, :, :2176].reshape(128, 2176)) + dot_nt(hg[1], wbuf[b, :, :, :, 2176:].reshape(128, 2176))
                fetch(g1, i + 2, FF)
            else:
                t = dot_nt(hg[0], v2[:, :2176]) + dot_nt(hg[1], v2[:, 2176:])
            dn[:, 128 * i : 128 * i + 128] = t
        return run

    def norm_back(values, gain):
        xhat, r = centred(values)
        e = dn[...]
        eg = e * gain
        m1 = jnp.sum(eg, axis=-1, keepdims=True) * (1.0 / REAL)
        m2 = jnp.sum(eg * xhat, axis=-1, keepdims=True) * (1.0 / REAL)
        back = jnp.where(iota((1, WIDE), 1) < REAL, r * (eg - m1 - xhat * m2), 0.0)
        return back, jnp.sum(e * xhat, axis=0, keepdims=True), jnp.sum(e, axis=0, keepdims=True)

    def total(t):
        return jnp.sum(t.astype(F32), axis=0, keepdims=True)

    def second_norm():
        back, gain_sum, shift_sum = norm_back(resid[...], vecs[5:6, :])
        t = cot[...].astype(F32) + back
        rgrad[...] = t
        low = t.astype(BF16)
        r1[1, :, WIDE:] = low
        small[4:5, :] = total(low)
        small[5:6, :] = gain_sum
        small[6:7, :] = shift_sum
        small[7:8, :] = total(cot[...])

    wo_copy = pltpu.make_async_copy(g0.at[:, :, :, :, :, pl.ds(3 * WIDE, WIDE)], wo, wsem.at[2])
    wo_copy.start()

    def attended_back():
        wo_copy.wait()
        low = r1[1, :, WIDE:]
        a = jnp.concatenate([dot_nt(low, wo[...].reshape(1024, WIDE)), dot_nt(low, v1[:, 3 * WIDE :])], axis=1).astype(BF16)
        gh[...] = dot_nt(a, perm[...]).astype(BF16)

    def attention_back(pair):
        def run():
            lanes = pl.ds(128 * pair, 128)
            q, k, v, g = qkv[0, :, lanes], qkv[1, :, lanes], qkv[2, :, lanes], gh[:, lanes]
            low_half = iota((1, 128), 1) < 64
            dq = jnp.zeros((TOK, 128), F32)
            dk, dv = dq, dq
            for half in range(2):
                mask = low_half if half == 0 else jnp.logical_not(low_half)
                pick = lambda t: jnp.where(mask, t, jnp.zeros_like(t))
                qh, kh, vh, gg = pick(q), pick(k), pick(v), pick(g)
                sc = dot_nt(q, kh) * 0.125 + bias[0]
                e = jnp.exp(sc - jnp.max(sc, axis=1, keepdims=True))
                p = e / jnp.sum(e, axis=1, keepdims=True)
                dp = dot_nt(g, vh)
                ds = (p * (dp - jnp.sum(p * dp, axis=1, keepdims=True))).astype(BF16)
                dq = dq + dot(ds, kh)
                sc = dot_nt(k, qh) * 0.125 + bias[1]
                e = jnp.exp(sc - jnp.max(sc, axis=0, keepdims=True))
                p = e / jnp.sum(e, axis=0, keepdims=True)
                dp = dot_nt(v, gg)
                ds = (p * (dp - jnp.sum(p * dp, axis=0, keepdims=True))).astype(BF16)
                dk = dk + dot(ds, qh)
                dv = dv + dot(p.astype(BF16), gg)
            lo = 128 * pair
            dq, dk, dv = (dq * 0.125).astype(BF16), (dk * 0.125).astype(BF16), dv.astype(BF16)
            r1[0, :, lo : lo + 128] = dq
            r1[0, :, WIDE + lo : WIDE + lo + 128] = dk
            r1[1, :, lo : lo + 128] = dv
            small[2:3, lo : lo + 128] = total(dq)
            small[3:4, lo : lo + 128] = total(dv)
        return run

    def give_first():
        give(6, r1.at[other], sr1)

    def first_norm_part(i):
        def run():
            if i == 0:
                fetch(g0, 0, 3 * WIDE)
                fetch(g0, 1, 3 * WIDE)
            if i < 8:
                fetched[i].wait()
                b = i % 2
                t = dot_nt(r1[0], wbuf[b, :, :, :, :2304].reshape(128, 2304)) + dot_nt(r1[1, :, :WIDE], wbuf[b, :, :, :, 2304:3456].reshape(128, WIDE))
                fetch(g0, i + 2, 3 * WIDE)
            else:
                t = dot_nt(r1[0], v1[:, :2304]) + dot_nt(r1[1, :, :WIDE], v1[:, 2304:3456])
            dn[:, 128 * i : 128 * i + 128] = t
        return run

    def first_norm():
        back, gain_sum, shift_sum = norm_back(tokens[...].astype(F32), vecs[0:1, :])
        rgrad[...] = rgrad[...] + back
        small[0:1, :] = gain_sum
        small[1:2, :] = shift_sum

    def natural_grad():
        t = rgrad[...]
        high = t.astype(BF16)
        t = t - high.astype(F32)
        mid = t.astype(BF16)
        low = (t - mid.astype(F32)).astype(BF16)
        grad[...] = dot_nt(high, perm[...]) + dot_nt(mid, perm[...]) + dot_nt(low, perm[...])

    def left_rows(t):
        def run():
            def put(i, values):
                left[i // 16, pl.ds(i % 16, 32, stride=16), :] = values

            tail = pl.ds(1024, 64)
            for j in range(9):
                lane = 512 * j + 128 * t
                rhs = r1[0, :, lane : lane + 128] if lane < 2304 else r1[1, :, lane - 2304 : lane - 2176]
                v = dot(lt[1 if lane >= 3 * WIDE else 0, tail, :], rhs)
                put(j, v[:32])
                put(9 + j, v[32:])
                if lane < FF:
                    rhs = hg[0, :, lane : lane + 128] if lane < 2176 else hg[1, :, lane - 2176 : lane - 2048]
                    v = dot(nst[tail, :], rhs)
                else:
                    v = jnp.zeros((64, 128), F32)
                put(18 + j, v[:32])
                put(27 + j, v[32:])
            for j in range(3):
                lane = 512 * j + 128 * t
                for b in range(2):
                    v = dot(actt[32 + b].reshape(128, TOK), cot[:, lane : lane + 128]) if lane < WIDE else jnp.zeros((128, 128), F32)
                    for i in range(4):
                        put(36 + 3 * (4 * b + i) + j, v[32 * i : 32 * i + 32])
            pick, own = dealt_pick()
            for i in range(2):
                v = small[4 * i + t : 4 * i + t + 1, :].astype(BF16)
                if i == 0 and t >= 2:
                    v = dot(v, perm[...]).astype(BF16)
                put(60 + i, dot_nt((own * v.astype(F32)).astype(BF16), pick))
            pick, own = hidden_pick(t)
            v = jnp.concatenate([total(hg[0]), total(hg[1])], axis=1)
            put(62, dot_nt((own * v).astype(BF16), pick))
            put(63, jnp.zeros((32, 128), F32))
            for zl in range(2):
                sums[3][:, :, :, zl, :, 128 * t : 128 * t + 128] = left[2 * zl + core].reshape(2, 4, 4, 16, 128).astype(BF16)
                pr[:, :, :, zl, :, 128 * t : 128 * t + 128] = left[2 * zl + other].reshape(2, 4, 4, 16, 128).astype(BF16)
        return run

    def give_left():
        give(7, pr, spr)

    def take_left():
        exchange[7].wait_recv()
        def body(zh, x, i):
            sums[3][zh, x] = (sums[3][zh, x].astype(F32) + spr[zh, x].astype(F32)).astype(BF16)
        over_blocks(body)

    C = lambda c, k: (lambda: comm(c, k))
    n2 = [second_norm_part(i) for i in range(9)]
    at_ = [attention_back(i) for i in range(9)]
    n1 = [first_norm_part(i) for i in range(9)]
    script = [down_weight, C(0, 0), up_weight, C(1, 0)] + n2 + [second_norm, C(0, 1), attended_back, C(1, 1)]
    script += at_[:3] + [C(0, 2)] + at_[3:6] + [C(1, 2)] + at_[6:] + [give_first, C(0, 3), C(1, 3)]
    script += [first_weight, C(2, 0)] + n1[:5] + [C(0, 4), C(1, 4)] + n1[5:] + [first_norm] + [left_rows(t) for t in range(4)] + [give_left]
    script += [C(2, 1), C(0, 5), C(1, 5), take_left, C(3, 0), natural_grad, C(2, 2), C(0, 6), C(1, 6), C(3, 1), C(2, 3), C(3, 2)]
    script += [C(2, 4), C(3, 3), C(2, 5), C(3, 4), C(2, 6), C(3, 5), C(3, 6), C(0, 7), C(1, 7), C(2, 7), C(3, 7)]
    for f in script:
        f()
    for c in local:
        c.wait()
    for c in pending:
        c.wait_send()
    for u in range(len(U)):
        for phase in range(3):
            sent(u, phase)


def backward_call(*ops):
    U = scatter_units()
    V, D, S = pltpu.VMEM, pltpu.SemaphoreType.DMA, jax.ShapeDtypeStruct
    here, vm = pl.BlockSpec(memory_space=pl.ANY), pl.BlockSpec(memory_space=pltpu.VMEM)
    scratch = [V((2, 4, 4, 2, 16, 2304), BF16), V((2, 4, 4, 2, 16, 2176), BF16), V((2, 4, 4, 2, 32, WIDE), BF16), V((2, 4, 4, 2, 16, 512), BF16)]
    scratch += [V((32, 2, 32, TOK), BF16), V((TOK, WIDE), BF16), V((WIDE, TOK), BF16), V((TOK, 2176), BF16), V((WIDE, TOK), BF16), V((WIDE, TOK), BF16)]
    scratch += [V((TOK, 2304), BF16), V((2, 4, 4, 2, 16, 512), BF16)]
    scratch += [V((2, 4, 2, 16, FF), BF16), V((2, 4, 4, 2, 16, WIDE), BF16), V((TOK, WIDE), F32), V((TOK, WIDE), F32), V((2, TOK, 2304), BF16)]
    scratch += [V((TOK, WIDE), BF16), V((4, 512, 128), F32), V((2, 4, 4, 2, 16, 512), BF16), V((8, WIDE), F32)]
    for w, g, c0, h0, h1 in U:
        for p in range(3):
            dims = block_dims(ORDERS[g][::-1], p)
            scratch += [V((3,) + dims + (ROWS[w], h0), BF16), V((3,) + dims + (ROWS[w], h1), BF16)]
    n = len(U)
    scratch += [D((n, 3, 2)), D((n, 3, 4)), D((8,)), D((8,)), D((n, 3)), D((n, 3)), D((n,)), D((3,))]
    scratch += [V(o.shape, o.dtype) for o in ops[2:]] + [D((13,))]
    return pl.pallas_call(
        backward_kernel,
        out_shape=(S((2, 16, 4608), BF16), S((2, 16, FF), BF16), S((2, 2, 32, WIDE), BF16), S((2, 2, 16, 512), BF16), S((TOK, WIDE), F32)),
        in_specs=[here] * 15,
        out_specs=(here,) * 4 + (vm,),
        scratch_shapes=scratch,
        compiler_params=pltpu.CompilerParams(collective_id=1, has_side_effects=True, vmem_limit_bytes=63 * 2**20),
    )(*ops)


def body(*args):
    pieces, tokens, cot, perm, turn, bias = prepare(*args)
    g0, g1, g2, g3, v1, v2, vecs, lt, nst, actt, qkv, resid, hg, layer_out = forward_call(*pieces, tokens, cot, perm, bias)
    both = jnp.stack([bias, bias.T])
    s0, s1, s2, s3, grad = backward_call(g0, g1, v1, v2, vecs, lt, nst, actt, qkv, resid, hg, tokens, cot, perm, both)
    left = s3.reshape(64, 512)
    first = jnp.concatenate([s0.reshape(32, 4608), left[:18].reshape(2, 4608)], axis=0)
    up_d = jnp.concatenate([s1.reshape(32, FF), left[18:36].reshape(2, 4608)[:, :FF]], axis=0)
    up_left = dot_nt(up_d[:, 4096:], turn).astype(BF16).reshape(34, 4, 64)
    up_d = widen(jnp.concatenate([up_d[:, :4096].reshape(34, 4, 1024), up_left], axis=2))
    down_d = jnp.concatenate([s2.reshape(4, 32, WIDE), left[36:60].reshape(4, 2, 1536)[:, :, :WIDE]], axis=1)
    stacked = jnp.concatenate([first[:, 3 * WIDE :], up_d.reshape(136, WIDE), down_d.reshape(136, WIDE)], axis=0)
    stacked = dot_nt(stacked, perm[:REAL])
    small = left[60:62].reshape(8, 128)[:, :34].astype(F32)
    units = left[62].reshape(4, 128)[:, :34].reshape(136).astype(F32)
    qkv_grad = first[:, : 3 * WIDE].reshape(34, 3, WIDE)[:, :, :REAL].reshape(34, 3 * REAL).astype(F32)
    return (
        layer_out[:, :REAL], grad[:, :REAL], small[0], small[1], qkv_grad, small[2], small[3], stacked[:34], small[4],
        small[5], small[6], stacked[34:170].reshape(34, FF), units, stacked[170:], small[7],
    )


def solution(mesh):
    ins, outs = specs()
    return jax.shard_map(body, mesh=mesh, in_specs=ins, out_specs=outs, check_vma=False)
```
